32 devices in a mesh: space: 16 (over z, x, core), chan: 2 (over y).
Axes of the slice: x: 2, y: 2, z: 4, core: 2. Of those that a mesh axis runs over, the one named last changes fastest.
Arguments:
- volume: bfloat16 [64, 16, 48, 128], P('chan', 'space'), may hold values from -6 to 6
- weight: bfloat16 [64, 64, 3, 3, 3], P('chan'), may hold values from -0.15625 to 0.15625
- bias: float32 [64], P('chan'), may hold values from -3 to 3
- upstream: bfloat16 [64, 16, 48, 128], P('chan', 'space'), may hold values from -6 to 6
Outputs:
- activated: bfloat16 [64, 16, 48, 128], P('chan', 'space')
- input_grad: bfloat16 [64, 16, 48, 128], P('chan', 'space')
- weight_grad: float32 [64, 64, 3, 3, 3], P('chan')
- bias_grad: float32 [64], P('chan')
The draws below stay inside these ranges and needn't reach their ends.
All inputs are finite; a program needn't handle non-finite values.
Results may differ from the reference program's by a relative error of at most 0.008.
Values may be sent and summed in bfloat16 or wider, within the bound.
No kernel may reach another device: no remote copies, remote signals or barrier semaphores. Data moves between devices by JAX's collectives and lax.ppermute only.
A program may use at most 64 MiB of HBM per device.

```python
import math
import jax
import jax.numpy as jnp
from jax import lax

CH = 64
HR = 48
WD = 128
DEPTH = 16


def levels(key, extent, split, least, top_value):
    loudness = 1.0
    for position, blocks in split:
        draws = jax.random.uniform(jax.random.fold_in(jax.random.fold_in(key, 6), position), (blocks,), jnp.float32, least / len(split), top_value / len(split))
        loudness = loudness * jnp.repeat(jnp.exp(draws), extent[position] // blocks).reshape((-1,) + (1,) * (len(extent) - 1 - position))
    return loudness


def bell_draw(own_key, shape, spread, bound, cuts=(), kind=jnp.bfloat16):
    loudness = levels(own_key, shape, cuts, -0.22, 0.18) if cuts else 1.0
    values = jax.random.normal(own_key, shape, jnp.float32) * spread * loudness
    return jnp.minimum(jnp.maximum(values, -bound), bound).astype(kind)


def setup_inputs(seed: int = 0) -> dict:
    key_of = jax.random.split(jax.random.key(seed), 5)
    volume = bell_draw(key_of[0], (CH, DEPTH, HR, WD), 1.0, 6.0, ((0, 2), (1, 16)))
    weight = bell_draw(key_of[1], (CH, CH, 3, 3, 3), (CH * 27) ** -0.5, 0.15625, ((0, 2),))
    bias = bell_draw(key_of[2], (CH,), 0.5, 3.0, ((0, 2),), jnp.float32)
    upstream = bell_draw(key_of[3], (CH, DEPTH, HR, WD), 1.0, 6.0, ((0, 2), (1, 16)))
    return dict(volume=volume, weight=weight, bias=bias, upstream=upstream)


leakage = 0.1

def convolve(lhs, rhs, padding):
    return lax.conv_general_dilated(lhs, rhs, (1, 1, 1), padding, dimension_numbers=('NCDHW', 'OIDHW', 'NCDHW'), preferred_element_type=jnp.float32)

def reference(volume, weight, bias, upstream):
    padding = [(1, 1), (1, 1), (1, 1)]
    preact = convolve(volume[None], weight, padding)[0] + bias[:, None, None, None].astype(jnp.float32)
    activated = (leakage * preact + (1.0 - leakage) * jax.nn.softplus(preact)).astype(jnp.bfloat16)
    delta = (upstream.astype(jnp.float32) * (leakage + (1.0 - leakage) * jax.nn.sigmoid(preact))).astype(jnp.bfloat16)
    flipped = jnp.transpose(weight, (1, 0, 2, 3, 4))[:, :, ::-1, ::-1, ::-1]
    input_grad = convolve(delta[None], flipped, padding)[0].astype(jnp.bfloat16)
    factor = 1.0 / math.sqrt(DEPTH * HR * WD)
    summed = convolve(volume[:, None], delta[:, None], padding)
    weight_grad = jnp.transpose(summed, (1, 0, 2, 3, 4)) * factor
    bias_grad = lax.optimization_barrier(jnp.sum(delta.astype(jnp.float32), axis=(1, 2, 3))) * factor
    return (activated, input_grad, weight_grad, bias_grad)
```

```python
import functools
import math

import jax
import jax.numpy as jnp
from jax import lax
from jax.experimental import pallas as pl
from jax.experimental.pallas import tpu as pltpu
from jax.sharding import PartitionSpec as P

leakage = 0.1
bf16 = jnp.bfloat16
f32 = jnp.float32
LIMIT = 48 * 1024 * 1024


def call(body, out_shape, scratch, flops, nbytes, trans=0, name=None):
    return pl.pallas_call(
        body,
        out_shape=out_shape,
        scratch_shapes=scratch,
        compiler_params=pltpu.CompilerParams(vmem_limit_bytes=LIMIT),
        cost_estimate=pl.CostEstimate(
            flops=flops, bytes_accessed=nbytes, transcendentals=trans
        ),
        name=name,
    )


def shape(*dims, dtype=bf16):
    return jax.ShapeDtypeStruct(dims, dtype)


def tap(a, b, c):
    return (a * 3 + b) * 3 + c


def pack_body(nchan, rows, height, *refs):
    vol, up, w, bias, v_own, u_own = refs[:6]
    v_out = refs[6 : 6 + nchan - 1]
    u_out = refs[6 + nchan - 1 : 6 + 2 * (nchan - 1)]
    flat, vt, ut = refs[6 + 2 * (nchan - 1) :]
    share = vol.shape[0]
    part = lax.axis_index("chan")
    zero = jnp.zeros((2, share, 128), bf16)
    for src, dst, rim in ((vol, vt, 2), (up, ut, 1)):
        flat[...] = src[...].astype(f32).reshape(share * height, 128)
        dst[0:rim] = zero[:rim]
        dst[height + rim : height + 2 * rim] = zero[:rim]
        for h in range(height):
            dst[h + rim] = flat[pl.ds(h, share, stride=height)].astype(bf16)
    lane = lax.broadcasted_iota(jnp.int32, (share, 64), 1)
    b = bias[...]
    b0 = b.astype(bf16).astype(f32)
    b1 = (b - b0).astype(bf16).astype(f32)
    b2 = b - b0 - b1
    pieces = jnp.where(
        lane == 0, b0, jnp.where(lane == 1, b1, jnp.where(lane == 2, b2, 0.0))
    )
    none = jnp.zeros((share, 64), f32)
    packed = []
    for c in range(3):
        for j in range(5):
            halves = []
            for t in (2 * j, 2 * j + 1):
                if t < 9:
                    halves.append(w[tap(t % 3, t // 3, c)].astype(f32))
                else:
                    halves.append(pieces if c == 1 else none)
            packed.append(jnp.concatenate(halves, axis=1).astype(bf16))
    v_own[...] = vt[pl.ds(part * rows, rows + 4)]
    u_own[0 : rows + 2] = ut[pl.ds(part * rows, rows + 2)]
    for n, value in enumerate(packed):
        u_own[rows + 2 + n] = value
    for k in range(1, nchan):
        other = lax.rem(part + k, nchan)
        v_out[k - 1][...] = vt[pl.ds(other * rows, rows + 4)]
        u_out[k - 1][0 : rows + 2] = ut[pl.ds(other * rows, rows + 2)]
        for n, value in enumerate(packed):
            u_out[k - 1][rows + 2 + n] = value


def filters_body(nchan, rows, *refs):
    own = refs[0]
    got = refs[1:nchan]
    forward, backward = refs[nchan : nchan + 2]
    wall, turned = refs[nchan + 2 :]
    share = own.shape[1]
    part = lax.axis_index("chan")
    wall[part] = own[rows + 2 :]
    for k in range(1, nchan):
        wall[lax.rem(part + nchan - k, nchan)] = got[k - 1][rows + 2 :]
    full = nchan * share
    for c in range(3):
        for j in range(5):
            block = wall[:, c * 5 + j].reshape(full, 128)
            forward[c * full : (c + 1) * full, j * 128 : (j + 1) * 128] = block
    turned[...] = jnp.zeros_like(turned)
    for b in range(3):
        for a in range(3):
            s = b * 3 + a
            t = (2 - b) * 3 + (2 - a)
            for c in range(3):
                block = wall[:, (2 - c) * 5 + t // 2].reshape(full, 128).astype(f32)
                half = block[:, (t % 2) * 64 : (t % 2) * 64 + 64]
                turned[s * 64 : (s + 1) * 64, c * 64 : (c + 1) * 64] = half
    backward[...] = turned[...].T[: 3 * 64].astype(bf16)


def gather_planes(nchan, planes, own, mine, sib, pair):
    part = lax.axis_index("chan")
    even = lax.rem(lax.axis_index("space"), 2) == 0
    at_sib = jnp.where(even, 2, 0)
    at_pair = jnp.where(even, 0, 2)
    for place, blocks in ((1, own), (at_sib, sib), (at_pair, pair)):
        for k in range(nchan):
            planes[:, place, lax.rem(part + nchan - k, nchan)] = blocks[k][...]


def ones_rows(width):
    row = lax.broadcasted_iota(jnp.int32, (64, width), 0)
    return jnp.where(row < 3, 1.0, 0.0).astype(bf16)


def taps_of(planes, r, extra):
    block = planes[r : r + 3].reshape(-1, 128)
    return jnp.concatenate([block, extra], axis=0)


def shift_sum(y, full):
    lane = lax.broadcasted_iota(jnp.int32, (full, 128), 1)
    left = jnp.where(lane == 0, 0.0, pltpu.roll(y[:full], 1, 1))
    right = jnp.where(lane == 127, 0.0, pltpu.roll(y[2 * full :], 127, 1))
    return y[full : 2 * full] + left + right


def forward_body(nchan, rows, *refs):
    own, sib, pair = refs[:nchan], refs[nchan : 2 * nchan], refs[2 * nchan : 3 * nchan]
    ups = refs[3 * nchan : 4 * nchan]
    filters = refs[4 * nchan]
    outs = refs[4 * nchan + 1 : 5 * nchan + 1]
    delta = refs[5 * nchan + 1]
    planes, upstream, activated = refs[5 * nchan + 2 :]
    part = lax.axis_index("chan")
    share = own[0].shape[1]
    full = nchan * share
    gather_planes(nchan, planes, own, None, sib, pair)
    for k in range(nchan):
        upstream[:, lax.rem(part + nchan - k, nchan)] = ups[k][0 : rows + 2]
    extra = ones_rows(128)
    w = filters[...]
    for g in range((rows + 2) // 2):
        rhs = jnp.concatenate(
            [taps_of(planes, 2 * g, extra), taps_of(planes, 2 * g + 1, extra)], axis=1
        )
        y = jnp.dot(w, rhs, preferred_element_type=f32)
        for n in range(2):
            r = 2 * g + n
            v = shift_sum(y[:, n * 128 : (n + 1) * 128], full)
            e = jnp.exp(-jnp.abs(v))
            inv = 1.0 / (1.0 + e)
            sig = jnp.where(v >= 0, 1.0, e) * inv
            u = upstream[r].reshape(full, 128).astype(f32)
            delta[r] = (u * (leakage + (1.0 - leakage) * sig)).astype(bf16)
            if 1 <= r <= rows:
                soft = jnp.maximum(v, 0.0) + jnp.log(1.0 + e)
                act = (leakage * v + (1.0 - leakage) * soft).astype(bf16)
                activated[r - 1] = act.reshape(nchan, share, 128)
    for k in range(nchan):
        outs[k][...] = activated[:, lax.rem(part + k, nchan)]


def wgrad_body(nchan, rows, step, *refs):
    own, sib, pair = refs[:nchan], refs[nchan : 2 * nchan], refs[2 * nchan : 3 * nchan]
    delta = refs[3 * nchan]
    outs = refs[3 * nchan + 1 : 4 * nchan + 1]
    planes, acc = refs[4 * nchan + 1 :]
    part = lax.axis_index("chan")
    share = own[0].shape[1]
    full = nchan * share
    gather_planes(nchan, planes, own, None, sib, pair)
    extra = ones_rows(128)
    lane = lax.broadcasted_iota(jnp.int32, (full, 128), 1)
    total = None
    for g in range(rows // step):
        lhs, rhs = [], []
        for r in range(g * step + 1, (g + 1) * step + 1):
            d = delta[r].astype(f32)
            before = jnp.where(lane == 127, 0.0, pltpu.roll(d, 127, 1))
            after = jnp.where(lane == 0, 0.0, pltpu.roll(d, 1, 1))
            lhs.append(
                jnp.concatenate([before.astype(bf16), delta[r], after.astype(bf16)], axis=0)
            )
            rhs.append(taps_of(planes, r, extra))
        term = lax.dot_general(
            jnp.concatenate(lhs, axis=1),
            jnp.concatenate(rhs, axis=1),
            (((1,), (1,)), ((), ())),
            preferred_element_type=f32,
        )
        total = term if total is None else total + term
    acc[...] = total
    for k in range(nchan):
        q = lax.rem(part + k, nchan)
        for c in range(3):
            outs[k][c * share : (c + 1) * share] = acc[
                pl.ds(pl.multiple_of(c * full + q * share, 8), share)
            ].astype(outs[k].dtype)


def backward_body(nchan, rows, *refs):
    own, sib, pair, filters = refs[:4]
    outs = refs[4 : 4 + nchan]
    planes, result = refs[4 + nchan :]
    part = lax.axis_index("chan")
    share = outs[0].shape[1]
    full = nchan * share
    even = lax.rem(lax.axis_index("space"), 2) == 0
    planes[:, 1] = own[...]
    planes[:, jnp.where(even, 2, 0)] = sib[...]
    planes[:, jnp.where(even, 0, 2)] = pair[...]
    extra = jnp.zeros((64, 128), bf16)
    w = filters[...]
    for g in range(rows // 2):
        rhs = jnp.concatenate(
            [taps_of(planes, 2 * g, extra), taps_of(planes, 2 * g + 1, extra)], axis=1
        )
        y = jnp.dot(w, rhs, preferred_element_type=f32)
        for n in range(2):
            v = shift_sum(y[:, n * 128 : (n + 1) * 128], full)
            result[2 * g + n] = v.astype(bf16).reshape(nchan, share, 128)
    for k in range(nchan):
        outs[k][...] = result[:, lax.rem(part + k, nchan)]


def unpack_body(nchan, rows, height, *refs):
    blocks = refs[:nchan]
    out, flat = refs[nchan:]
    share = out.shape[0]
    part = lax.axis_index("chan")
    size = rows * share
    for k in range(nchan):
        q = lax.rem(part + nchan - k, nchan)
        flat[pl.ds(pl.multiple_of(q * size, 8), size)] = (
            blocks[k][...].astype(f32).reshape(size, 128)
        )
    for ch in range(share):
        out[ch] = flat[pl.ds(ch, height, stride=share)].astype(bf16)


def finish_body(share, factor, a_ref, b_ref, out, bias):
    total = (a_ref[...].astype(f32) + b_ref[...].astype(f32)) * factor
    for a in range(3):
        for b in range(3):
            for c in range(3):
                t = b * 3 + a
                out[tap(a, b, c)] = total[c * share : (c + 1) * share, t * 64 : t * 64 + 64]
    col = total[share : 2 * share, 576:577]
    eye = lax.broadcasted_iota(jnp.int32, (share, share), 0) == lax.broadcasted_iota(
        jnp.int32, (share, share), 1
    )
    bias[...] = jnp.sum(jnp.where(eye, col, 0.0), axis=0, keepdims=True)


def shards(volume, weight, bias, upstream):
    nchan, nspace = lax.axis_size("chan"), lax.axis_size("space")
    share, depth, height, width = volume.shape
    assert depth == 1 and width == 128 and height % nchan == 0
    full = nchan * share
    rows = height // nchan
    factor = 1.0 / math.sqrt(nspace * depth * height * width)
    sib_perm = [(i, i ^ 1) for i in range(nspace)]
    pair_perm = [(i, i + 1) for i in range(1, nspace - 1, 2)]
    pair_perm += [(j, i) for i, j in pair_perm]

    def over_chan(blocks):
        got = []
        for k in range(1, nchan):
            perm = [(i, (i + k) % nchan) for i in range(nchan)]
            got.append(lax.ppermute(blocks[k - 1], "chan", perm))
        return got

    def to_sib(x):
        return lax.ppermute(x, "space", sib_perm)

    def to_pair(x):
        return lax.ppermute(x, "space", pair_perm)

    slabs = jnp.transpose(weight, (2, 3, 4, 0, 1)).reshape(27, share, full)
    block = share * height * width * 2
    v_shape = shape(rows + 4, share, 128)
    u_shape = shape(rows + 17, share, 128)
    packed = call(
        functools.partial(pack_body, nchan, rows, height),
        [v_shape, u_shape] + [v_shape] * (nchan - 1) + [u_shape] * (nchan - 1),
        [
            pltpu.VMEM((share * height, 128), f32),
            pltpu.VMEM((height + 4, share, 128), bf16),
            pltpu.VMEM((height + 2, share, 128), bf16),
        ],
        0,
        4 * block,
        name="pack",
    )(
        volume.reshape(share, height, width),
        upstream.reshape(share, height, width),
        slabs,
        bias.reshape(share, 1),
    )
    v_own, u_own = packed[:2]
    v_out, u_out = packed[2 : 1 + nchan], packed[1 + nchan :]
    v_got = over_chan(v_out)
    u_got = over_chan(u_out)
    mine = [v_own] + v_got
    sib = [to_sib(x) for x in mine]
    pair = [to_pair(x) for x in mine]
    w_forward, w_backward = call(
        functools.partial(filters_body, nchan, rows),
        [shape(3 * full, 640), shape(3 * full, 640)],
        [pltpu.VMEM((nchan, 15, share, 128), bf16), pltpu.VMEM((640, 256), f32)],
        0,
        1 << 20,
        name="filters",
    )(u_own, *u_got)
    planes = pltpu.VMEM((rows + 4, 3, nchan, share, 128), bf16)
    cells = rows * width
    a_shape = shape(rows, share, 128)
    *act, delta = call(
        functools.partial(forward_body, nchan, rows),
        [a_shape] * nchan + [shape(rows + 2, full, 128)],
        [
            planes,
            pltpu.VMEM((rows + 2, nchan, share, 128), bf16),
            pltpu.VMEM((rows, nchan, share, 128), bf16),
        ],
        2 * 27 * full * full * cells,
        6 * block,
        2 * full * cells,
        name="forward",
    )(*mine, *sib, *pair, u_own, *u_got, w_forward)
    d_sib, d_pair = to_sib(delta), to_pair(delta)
    step = 4 if rows % 4 == 0 else 1
    partial = call(
        functools.partial(wgrad_body, nchan, rows, step),
        [shape(3 * share, 640, dtype=f32)] + [shape(3 * share, 640)] * (nchan - 1),
        [planes, pltpu.VMEM((3 * full, 640), f32)],
        2 * 27 * full * full * cells,
        6 * block,
        name="wgrad",
    )(*mine, *sib, *pair, delta)
    act_got = over_chan(act[1:])
    total = partial[0]
    for term in over_chan(partial[1:]):
        total = total + term.astype(f32)
    hop = 1
    while True:
        sent = total.astype(bf16)
        came = lax.ppermute(sent, "space", [(i, i ^ hop) for i in range(nspace)])
        hop *= 2
        if hop >= nspace:
            break
        total = sent.astype(f32) + came.astype(f32)
    ig = call(
        functools.partial(backward_body, nchan, rows),
        [a_shape] * nchan,
        [
            pltpu.VMEM((rows + 2, 3, full, 128), bf16),
            pltpu.VMEM((rows, nchan, share, 128), bf16),
        ],
        2 * 27 * full * full * cells,
        6 * block,
        name="backward",
    )(delta, d_sib, d_pair, w_backward)
    ig_got = over_chan(ig[1:])

    def unpack(blocks, name):
        out = call(
            functools.partial(unpack_body, nchan, rows, height),
            shape(share, height, width),
            [pltpu.VMEM((height * share, 128), f32)],
            0,
            2 * block,
            name=name,
        )(*blocks)
        return out.reshape(share, 1, height, width)

    activated = unpack([act[0]] + act_got, "unpack_activated")
    input_grad = unpack([ig[0]] + ig_got, "unpack_input_grad")
    w_grad, b_grad = call(
        functools.partial(finish_body, share, factor),
        [shape(27, share, full, dtype=f32), shape(1, share, dtype=f32)],
        [],
        0,
        1 << 20,
        name="finish",
    )(sent, came)
    w_grad = jnp.transpose(w_grad.reshape(3, 3, 3, share, full), (3, 4, 0, 1, 2))
    return activated, input_grad, w_grad, b_grad.reshape(share)


def solution(mesh):
    placed = (
        P("chan", "space", None, None),
        P("chan", None, None, None, None),
        P("chan"),
        P("chan", "space", None, None),
    )
    return jax.shard_map(
        shards,
        mesh=mesh,
        in_specs=placed,
        out_specs=(
            P("chan", "space", None, None),
            P("chan", "space", None, None),
            P("chan", None, None, None, None),
            P("chan"),
        ),
        check_vma=False,
    )
```

```python
import functools
import math

import jax
import jax.numpy as jnp
from jax import lax
from jax.experimental import pallas as pl
from jax.experimental.pallas import tpu as pltpu
from jax.sharding import PartitionSpec as P

leakage = 0.1
bf16 = jnp.bfloat16
f32 = jnp.float32
DBAR = 0
IBAR = 9
ABAR = 9
UBAR = False
ZHOP = 2
GBAR = 9
VWRAP = True
VWRAP2 = True
DWRAP = False
LIMIT = 48 * 1024 * 1024


def call(body, out_shape, scratch, flops, nbytes, trans=0, name=None):
    return pl.pallas_call(
        body,
        out_shape=out_shape,
        scratch_shapes=scratch,
        compiler_params=pltpu.CompilerParams(vmem_limit_bytes=LIMIT),
        cost_estimate=pl.CostEstimate(
            flops=flops, bytes_accessed=nbytes, transcendentals=trans
        ),
        name=name,
    )


def shape(*dims, dtype=bf16):
    return jax.ShapeDtypeStruct(dims, dtype)


def tap(a, b, c):
    return (a * 3 + b) * 3 + c


def rows_first(src, flat, dst, rim):
    share, height, _ = src.shape
    zero = jnp.zeros((rim, share, 128), bf16)
    flat[...] = src[...].astype(f32).reshape(share * height, 128)
    dst[0:rim] = zero
    dst[height + rim : height + 2 * rim] = zero
    for h in range(height):
        dst[h + rim] = flat[pl.ds(h, share, stride=height)].astype(bf16)


def pack_volume_body(nchan, rows, *refs):
    vol = refs[0]
    outs = refs[1 : 1 + nchan]
    flat, vt = refs[1 + nchan :]
    part = lax.axis_index("chan")
    rows_first(vol, flat, vt, 2)
    for k in range(nchan):
        outs[k][...] = vt[pl.ds(lax.rem(part + k, nchan) * rows, rows + 4)]


def core():
    return lax.rem(lax.axis_index("space"), 2)


def pack_rest_body(nchan, rows, *refs):
    up, w, bias = refs[:3]
    outs = refs[3 : 3 + nchan]
    flat, ut = refs[3 + nchan :]
    share = up.shape[0]
    part = lax.axis_index("chan")
    rows_first(up, flat, ut, 1)
    lane = lax.broadcasted_iota(jnp.int32, (share, 64), 1)
    row = lax.broadcasted_iota(jnp.int32, (share, share), 0)
    col = lax.broadcasted_iota(jnp.int32, (share, share), 1)
    b = jnp.sum(jnp.where(row == col, bias[...], 0.0), axis=1, keepdims=True)
    b0 = b.astype(bf16).astype(f32)
    b1 = (b - b0).astype(bf16).astype(f32)
    b2 = b - b0 - b1
    pieces = jnp.where(
        lane == 0, b0, jnp.where(lane == 1, b1, jnp.where(lane == 2, b2, 0.0))
    )
    none = jnp.zeros((share, 64), f32)
    for c in range(3):
        for j in range(5):
            halves = []
            for t in (2 * j, 2 * j + 1):
                if t < 9:
                    halves.append(w[tap(t % 3, t // 3, c)].astype(f32))
                else:
                    halves.append(pieces if c == 1 else none)
            value = jnp.concatenate(halves, axis=1).astype(bf16)
            for k in range(nchan):
                outs[k][rows + 2 + c * 5 + j] = value
    for k in range(nchan):
        outs[k][0 : rows + 2] = ut[pl.ds(lax.rem(part + k, nchan) * rows, rows + 2)]


def filters_body(nchan, rows, *refs):
    blocks = refs[:nchan]
    forward, backward, wall, turned = refs[nchan:]
    share = blocks[0].shape[1]
    part = lax.axis_index("chan")
    for k in range(nchan):
        wall[lax.rem(part + nchan - k, nchan)] = blocks[k][rows + 2 :]
    full = nchan * share
    for c in range(3):
        for j in range(5):
            block = wall[:, c * 5 + j].reshape(full, 128)
            forward[c * full : (c + 1) * full, j * 128 : (j + 1) * 128] = block
    turned[...] = jnp.zeros_like(turned)
    for b in range(3):
        for a in range(3):
            s = b * 3 + a
            t = (2 - b) * 3 + (2 - a)
            for c in range(3):
                block = wall[:, (2 - c) * 5 + t // 2].reshape(full, 128).astype(f32)
                half = block[:, (t % 2) * 64 : (t % 2) * 64 + 64]
                turned[s * 64 : (s + 1) * 64, c * 64 : (c + 1) * 64] = half
    backward[...] = turned[...].T[: 3 * 64].astype(bf16)


def outermost():
    at = lax.axis_index("space")
    return (at == 0) | (at == lax.axis_size("space") - 1)


def gather_planes(nchan, planes, own, mine, sib, pair):
    part = lax.axis_index("chan")
    even = lax.rem(lax.axis_index("space"), 2) == 0
    at_sib = jnp.where(even, 2, 0)
    at_pair = jnp.where(even, 0, 2)
    for place, blocks in ((1, own), (at_sib, sib), (at_pair, pair)):
        for k in range(nchan):
            planes[:, place, lax.rem(part + nchan - k, nchan)] = blocks[k][...]

    @pl.when(outermost())
    def _():
        planes[:, at_pair] = jnp.zeros(planes[:, at_pair].shape, bf16)


def ones_rows(width):
    row = lax.broadcasted_iota(jnp.int32, (64, width), 0)
    return jnp.where(row < 3, 1.0, 0.0).astype(bf16)


def taps_of(planes, r, extra):
    block = planes[r : r + 3].reshape(-1, 128)
    return jnp.concatenate([block, extra], axis=0)


def shift_sum(y, full):
    lane = lax.broadcasted_iota(jnp.int32, (full, 128), 1)
    left = jnp.where(lane == 0, 0.0, pltpu.roll(y[:full], 1, 1))
    right = jnp.where(lane == 127, 0.0, pltpu.roll(y[2 * full :], 127, 1))
    return y[full : 2 * full] + left + right


def forward_body(nchan, rows, *refs):
    own, sib, pair = refs[:nchan], refs[nchan : 2 * nchan], refs[2 * nchan : 3 * nchan]
    ups = refs[3 * nchan : 4 * nchan]
    filters = refs[4 * nchan]
    outs = refs[4 * nchan + 1 : 5 * nchan + 1]
    delta = refs[5 * nchan + 1]
    planes, upstream, activated = refs[5 * nchan + 2 :]
    part = lax.axis_index("chan")
    share = own[0].shape[1]
    full = nchan * share
    gather_planes(nchan, planes, own, None, sib, pair)
    for k in range(nchan):
        upstream[:, lax.rem(part + nchan - k, nchan)] = ups[k][0 : rows + 2]
    extra = ones_rows(128)
    w = filters[...]
    for g in range((rows + 2) // 2):
        rhs = jnp.concatenate(
            [taps_of(planes, 2 * g, extra), taps_of(planes, 2 * g + 1, extra)], axis=1
        )
        y = jnp.dot(w, rhs, preferred_element_type=f32)
        for n in range(2):
            r = 2 * g + n
            v = shift_sum(y[:, n * 128 : (n + 1) * 128], full)
            e = jnp.exp(-jnp.abs(v))
            inv = 1.0 / (1.0 + e)
            sig = jnp.where(v >= 0, 1.0, e) * inv
            u = upstream[r].reshape(full, 128).astype(f32)
            delta[r] = (u * (leakage + (1.0 - leakage) * sig)).astype(bf16)
            if 1 <= r <= rows:
                soft = jnp.maximum(v, 0.0) + jnp.log(1.0 + e)
                act = (leakage * v + (1.0 - leakage) * soft).astype(bf16)
                activated[r - 1] = act.reshape(nchan, share, 128)
    for k in range(nchan):
        outs[k][...] = activated[:, lax.rem(part + k, nchan)]


def wgrad_body(nchan, rows, step, *refs):
    own, sib, pair = refs[:nchan], refs[nchan : 2 * nchan], refs[2 * nchan : 3 * nchan]
    delta = refs[3 * nchan]
    kept, sent, planes, acc = refs[3 * nchan + 1 :]
    part = lax.axis_index("chan")
    share = own[0].shape[1]
    full = nchan * share
    gather_planes(nchan, planes, own, None, sib, pair)
    extra = ones_rows(128)
    lane = lax.broadcasted_iota(jnp.int32, (full, 128), 1)
    total = None
    for g in range(rows // step):
        lhs, rhs = [], []
        for r in range(g * step + 1, (g + 1) * step + 1):
            d = delta[r].astype(f32)
            before = jnp.where(lane == 127, 0.0, pltpu.roll(d, 127, 1))
            after = jnp.where(lane == 0, 0.0, pltpu.roll(d, 1, 1))
            lhs.append(
                jnp.concatenate([before.astype(bf16), delta[r], after.astype(bf16)], axis=0)
            )
            rhs.append(taps_of(planes, r, extra))
        term = lax.dot_general(
            jnp.concatenate(lhs, axis=1),
            jnp.concatenate(rhs, axis=1),
            (((1,), (1,)), ((), ())),
            preferred_element_type=f32,
        )
        total = term if total is None else total + term
    for c in range(3):
        for q in range(nchan):
            at = (q * 3 + c) * share
            acc[at : at + share] = total[c * full + q * share : c * full + (q + 1) * share]
    half = 3 * share // 2
    for k in range(nchan):
        at = lax.rem(part + k, nchan) * 3 * share
        kept[k] = acc[pl.ds(pl.multiple_of(at + core() * half, 8), half)]
        sent[k] = acc[pl.ds(pl.multiple_of(at + (1 - core()) * half, 8), half)].astype(bf16)


def backward_body(nchan, rows, *refs):
    own, sib, pair, filters = refs[:4]
    outs = refs[4 : 4 + nchan]
    planes, result = refs[4 + nchan :]
    part = lax.axis_index("chan")
    share = outs[0].shape[1]
    full = nchan * share
    even = lax.rem(lax.axis_index("space"), 2) == 0
    planes[:, 1] = own[...]
    planes[:, jnp.where(even, 2, 0)] = sib[...]
    at_pair = jnp.where(even, 0, 2)
    planes[:, at_pair] = pair[...]

    @pl.when(outermost())
    def _():
        planes[:, at_pair] = jnp.zeros(pair.shape, bf16)

    extra = jnp.zeros((64, 128), bf16)
    w = filters[...]
    for g in range(rows // 2):
        rhs = jnp.concatenate(
            [taps_of(planes, 2 * g, extra), taps_of(planes, 2 * g + 1, extra)], axis=1
        )
        y = jnp.dot(w, rhs, preferred_element_type=f32)
        for n in range(2):
            v = shift_sum(y[:, n * 128 : (n + 1) * 128], full)
            result[2 * g + n] = v.astype(bf16).reshape(nchan, share, 128)
    for k in range(nchan):
        outs[k][...] = result[:, lax.rem(part + k, nchan)]


def unpack_body(nchan, rows, height, *refs):
    blocks = refs[:nchan]
    out, flat = refs[nchan:]
    share = out.shape[0]
    part = lax.axis_index("chan")
    size = rows * share
    for k in range(nchan):
        q = lax.rem(part + nchan - k, nchan)
        flat[pl.ds(pl.multiple_of(q * size, 8), size)] = (
            blocks[k][...].astype(f32).reshape(size, 128)
        )
    for ch in range(share):
        out[ch] = flat[pl.ds(ch, height, stride=share)].astype(bf16)


def finish_body(share, factor, mine, other, out, bias, both):
    half = 3 * share // 2
    both[pl.ds(pl.multiple_of(core() * half, 8), half)] = mine[...]
    both[pl.ds(pl.multiple_of((1 - core()) * half, 8), half)] = other[...]
    total = both[...] * factor
    for a in range(3):
        for b in range(3):
            for c in range(3):
                t = b * 3 + a
                out[tap(a, b, c)] = total[c * share : (c + 1) * share, t * 64 : t * 64 + 64]
    col = total[share : 2 * share, 576:577]
    eye = lax.broadcasted_iota(jnp.int32, (share, share), 0) == lax.broadcasted_iota(
        jnp.int32, (share, share), 1
    )
    bias[...] = jnp.sum(jnp.where(eye, col, 0.0), axis=0, keepdims=True)


def kept_sum(first, others):
    total = first.astype(f32)
    for term in others:
        total = total + term.astype(f32)
    return total


def shards(volume, weight, bias, upstream):
    nchan, nspace = lax.axis_size("chan"), lax.axis_size("space")
    share, depth, height, width = volume.shape
    assert depth == 1 and width == 128 and height % nchan == 0
    full = nchan * share
    rows = height // nchan
    factor = 1.0 / math.sqrt(nspace * depth * height * width)
    sib_perm = [(i, i ^ 1) for i in range(nspace)]
    pairs = [(i, i + 1) for i in range(1, nspace - 1, 2)]
    pairs += [(j, i) for i, j in pairs]
    pair_perm = [(i * nchan + c, j * nchan + c) for i, j in pairs for c in range(nchan)]
    ends = (0, nspace - 1)
    turn_perm = [
        (i * nchan + c, i * nchan + (c + 1) % nchan) for i in ends for c in range(nchan)
    ]
    wrap_perm = [
        (i * nchan + c, (nspace - 1 - i) * nchan + c) for i in ends for c in range(nchan)
    ]

    def over_chan(blocks):
        got = []
        for k in range(1, nchan):
            perm = [(i, (i + k) % nchan) for i in range(nchan)]
            got.append(lax.ppermute(blocks[k - 1], "chan", perm))
        return got

    def to_sib(x):
        return lax.ppermute(x, "space", sib_perm)

    def to_pair(x, wrap):
        perm = pair_perm + (wrap_perm if wrap else turn_perm)
        return lax.ppermute(x, ("space", "chan"), perm)

    slabs = jnp.transpose(weight, (2, 3, 4, 0, 1)).reshape(27, share, full)
    block = share * height * width * 2
    v_shape = shape(rows + 4, share, 128)
    u_shape = shape(rows + 17, share, 128)
    v_own, *v_out = call(
        functools.partial(pack_volume_body, nchan, rows),
        [v_shape] * nchan,
        [
            pltpu.VMEM((share * height, width), f32),
            pltpu.VMEM((height + 4, share, width), bf16),
        ],
        0,
        2 * block,
        name="pack_volume",
    )(volume.reshape(share, height, width))
    v_got = over_chan(v_out)
    own_sib, own_pair = to_sib(v_own), to_pair(v_own, VWRAP)
    u_own, *u_out = call(
        functools.partial(pack_rest_body, nchan, rows),
        [u_shape] * nchan,
        [
            pltpu.VMEM((share * height, width), f32),
            pltpu.VMEM((height + 2, share, width), bf16),
        ],
        0,
        3 * block,
        name="pack_rest",
    )(upstream.reshape(share, height, width), slabs, bias.reshape(1, share))
    if UBAR:
        u_out, v_got = lax.optimization_barrier((u_out, v_got))
    v_got, own_sib, own_pair = lax.optimization_barrier((v_got, own_sib, own_pair))
    mine = [v_own] + v_got
    sib = [own_sib] + [to_sib(x) for x in v_got]
    pair = [own_pair] + [to_pair(x, VWRAP2) for x in v_got]
    u_got = over_chan(u_out)
    w_forward, w_backward = call(
        functools.partial(filters_body, nchan, rows),
        [shape(3 * full, 640), shape(3 * full, 640)],
        [pltpu.VMEM((nchan, 15, share, 128), bf16), pltpu.VMEM((640, 256), f32)],
        0,
        1 << 20,
        name="filters",
    )(u_own, *u_got)
    planes = pltpu.VMEM((rows + 4, 3, nchan, share, 128), bf16)
    cells = rows * width
    a_shape = shape(rows, share, 128)
    *act, delta = call(
        functools.partial(forward_body, nchan, rows),
        [a_shape] * nchan + [shape(rows + 2, full, 128)],
        [
            planes,
            pltpu.VMEM((rows + 2, nchan, share, 128), bf16),
            pltpu.VMEM((rows, nchan, share, 128), bf16),
        ],
        2 * 27 * full * full * cells,
        6 * block,
        2 * full * cells,
        name="forward",
    )(*mine, *sib, *pair, u_own, *u_got, w_forward)
    d_sib, d_pair = to_sib(delta), to_pair(delta, DWRAP)
    step = 4 if rows % 4 == 0 else 1
    h_shape = (nchan, 3 * share // 2, 640)
    kept, sent = call(
        functools.partial(wgrad_body, nchan, rows, step),
        [shape(*h_shape, dtype=f32), shape(*h_shape)],
        [planes, pltpu.VMEM((3 * full, 640), f32)],
        2 * 27 * full * full * cells,
        6 * block,
        name="wgrad",
    )(*mine, *sib, *pair, delta)
    kept = kept + to_sib(sent).astype(f32)
    sent = [kept[k].astype(bf16) for k in range(nchan)]
    near = kept_sum(sent[0], over_chan(sent[1:]))
    far = [
        lax.ppermute(
            sent[k],
            ("space", "chan"),
            [
                (i * nchan + c, (i ^ 2 * ZHOP) * nchan + (c + k) % nchan)
                for i in range(nspace)
                for c in range(nchan)
            ],
        )
        for k in range(nchan)
    ]
    total = near + kept_sum(far[0], far[1:])
    def unpack(blocks, name):
        out = call(
            functools.partial(unpack_body, nchan, rows, height),
            shape(share, height, width),
            [pltpu.VMEM((height * share, 128), f32)],
            0,
            2 * block,
            name=name,
        )(*blocks)
        return out.reshape(share, 1, height, width)

    activated = unpack([act[0]] + over_chan(act[1:]), "unpack_activated")
    ig = call(
        functools.partial(backward_body, nchan, rows),
        [a_shape] * nchan,
        [
            pltpu.VMEM((rows + 2, 3, full, 128), bf16),
            pltpu.VMEM((rows, nchan, share, 128), bf16),
        ],
        2 * 27 * full * full * cells,
        6 * block,
        name="backward",
    )(delta, d_sib, d_pair, w_backward)
    ig_got = over_chan(ig[1:])
    hops = [1 << n for n in range(1, nspace.bit_length() - 1)]
    hops.remove(2 * ZHOP)
    for n, hop in enumerate(hops[1:] + hops[:1]):
        if n == DBAR:
            total, d_sib, d_pair = lax.optimization_barrier((total, d_sib, d_pair))
        if n == IBAR:
            total, ig = lax.optimization_barrier((total, ig))
        if n == GBAR:
            total, ig_got = lax.optimization_barrier((total, ig_got))
        if n == ABAR:
            total, activated = lax.optimization_barrier((total, activated))
        sent = total.astype(bf16)
        came = lax.ppermute(sent, "space", [(i, i ^ hop) for i in range(nspace)])
        total = sent.astype(f32) + came.astype(f32)
    summed = to_sib(total)

    input_grad = unpack([ig[0]] + ig_got, "unpack_input_grad")
    w_grad, b_grad = call(
        functools.partial(finish_body, share, factor),
        [shape(27, share, full, dtype=f32), shape(1, share, dtype=f32)],
        [pltpu.VMEM((3 * share, 640), f32)],
        0,
        1 << 20,
        name="finish",
    )(total, summed)
    w_grad = jnp.transpose(w_grad.reshape(3, 3, 3, share, full), (3, 4, 0, 1, 2))
    return activated, input_grad, w_grad, b_grad.reshape(share)


def solution(mesh):
    placed = (
        P("chan", "space", None, None),
        P("chan", None, None, None, None),
        P("chan"),
        P("chan", "space", None, None),
    )
    return jax.shard_map(
        shards,
        mesh=mesh,
        in_specs=placed,
        out_specs=(
            P("chan", "space", None, None),
            P("chan", "space", None, None),
            P("chan", None, None, None, None),
            P("chan"),
        ),
        check_vma=False,
    )
```

```python
import functools
import math

import jax
import jax.numpy as jnp
from jax import lax
from jax.experimental import pallas as pl
from jax.experimental.pallas import tpu as pltpu
from jax.sharding import PartitionSpec as P

leakage = 0.1
bf16 = jnp.bfloat16
f32 = jnp.float32
DBAR = 9
IBAR = 9
ABAR = 9
UBAR = False
ZHOP = 2
GBAR = 9
SBAR = False
FLIP = True
VWRAP = True
VWRAP2 = True
DWRAP = False
LIMIT = 48 * 1024 * 1024


def call(body, out_shape, scratch, flops, nbytes, trans=0, name=None):
    return pl.pallas_call(
        body,
        out_shape=out_shape,
        scratch_shapes=scratch,
        compiler_params=pltpu.CompilerParams(vmem_limit_bytes=LIMIT),
        cost_estimate=pl.CostEstimate(
            flops=flops, bytes_accessed=nbytes, transcendentals=trans
        ),
        name=name,
    )


def shape(*dims, dtype=bf16):
    return jax.ShapeDtypeStruct(dims, dtype)


def tap(a, b, c):
    return (a * 3 + b) * 3 + c


def rows_first(src, flat, dst, rim):
    share, height, _ = src.shape
    zero = jnp.zeros((rim, share, 128), bf16)
    flat[...] = src[...].astype(f32).reshape(share * height, 128)
    dst[0:rim] = zero
    dst[height + rim : height + 2 * rim] = zero
    for h in range(height):
        dst[h + rim] = flat[pl.ds(h, share, stride=height)].astype(bf16)


def pack_volume_body(nchan, rows, *refs):
    vol = refs[0]
    outs = refs[1 : 1 + nchan]
    flat, vt = refs[1 + nchan :]
    part = lax.axis_index("chan")
    rows_first(vol, flat, vt, 2)
    for k in range(nchan):
        outs[k][...] = vt[pl.ds(lax.rem(part + k, nchan) * rows, rows + 4)]


def core():
    return lax.rem(lax.axis_index("space"), 2)


def pack_rest_body(nchan, rows, *refs):
    up, w, bias = refs[:3]
    outs = refs[3 : 3 + nchan]
    flat, ut = refs[3 + nchan :]
    share = up.shape[0]
    part = lax.axis_index("chan")
    rows_first(up, flat, ut, 1)
    lane = lax.broadcasted_iota(jnp.int32, (share, 64), 1)
    row = lax.broadcasted_iota(jnp.int32, (share, share), 0)
    col = lax.broadcasted_iota(jnp.int32, (share, share), 1)
    b = jnp.sum(jnp.where(row == col, bias[...], 0.0), axis=1, keepdims=True)
    b0 = b.astype(bf16).astype(f32)
    b1 = (b - b0).astype(bf16).astype(f32)
    b2 = b - b0 - b1
    pieces = jnp.where(
        lane == 0, b0, jnp.where(lane == 1, b1, jnp.where(lane == 2, b2, 0.0))
    )
    none = jnp.zeros((share, 64), f32)
    for c in range(3):
        for j in range(5):
            halves = []
            for t in (2 * j, 2 * j + 1):
                if t < 9:
                    halves.append(w[tap(t % 3, t // 3, c)].astype(f32))
                else:
                    halves.append(pieces if c == 1 else none)
            value = jnp.concatenate(halves, axis=1).astype(bf16)
            for k in range(nchan):
                outs[k][rows + 2 + c * 5 + j] = value
    for k in range(nchan):
        outs[k][0 : rows + 2] = ut[pl.ds(lax.rem(part + k, nchan) * rows, rows + 2)]


def filters_body(nchan, rows, *refs):
    blocks = refs[:nchan]
    forward, backward, wall, turned = refs[nchan:]
    share = blocks[0].shape[1]
    part = lax.axis_index("chan")
    for k in range(nchan):
        wall[lax.rem(part + nchan - k, nchan)] = blocks[k][rows + 2 :]
    full = nchan * share
    for c in range(3):
        for j in range(5):
            block = wall[:, c * 5 + j].reshape(full, 128)
            forward[c * full : (c + 1) * full, j * 128 : (j + 1) * 128] = block
    turned[...] = jnp.zeros_like(turned)
    for b in range(3):
        for a in range(3):
            s = b * 3 + a
            t = (2 - b) * 3 + (2 - a)
            for c in range(3):
                block = wall[:, (2 - c) * 5 + t // 2].reshape(full, 128).astype(f32)
                half = block[:, (t % 2) * 64 : (t % 2) * 64 + 64]
                turned[s * 64 : (s + 1) * 64, c * 64 : (c + 1) * 64] = half
    backward[...] = turned[...].T[: 3 * 64].astype(bf16)


def outermost():
    at = lax.axis_index("space")
    return (at == 0) | (at == lax.axis_size("space") - 1)


def gather_planes(nchan, planes, own, mine, sib, pair):
    part = lax.axis_index("chan")
    even = lax.rem(lax.axis_index("space"), 2) == 0
    at_sib = jnp.where(even, 2, 0)
    at_pair = jnp.where(even, 0, 2)
    for place, blocks in ((1, own), (at_sib, sib), (at_pair, pair)):
        for k in range(nchan):
            planes[:, place, lax.rem(part + nchan - k, nchan)] = blocks[k][...]

    @pl.when(outermost())
    def _():
        planes[:, at_pair] = jnp.zeros(planes[:, at_pair].shape, bf16)


def ones_rows(width):
    row = lax.broadcasted_iota(jnp.int32, (64, width), 0)
    return jnp.where(row < 3, 1.0, 0.0).astype(bf16)


def taps_of(planes, r, extra):
    block = planes[r : r + 3].reshape(-1, 128)
    return jnp.concatenate([block, extra], axis=0)


def shift_sum(y, full):
    lane = lax.broadcasted_iota(jnp.int32, (full, 128), 1)
    left = jnp.where(lane == 0, 0.0, pltpu.roll(y[:full], 1, 1))
    right = jnp.where(lane == 127, 0.0, pltpu.roll(y[2 * full :], 127, 1))
    return y[full : 2 * full] + left + right


def forward_body(nchan, rows, *refs):
    own, sib, pair = refs[:nchan], refs[nchan : 2 * nchan], refs[2 * nchan : 3 * nchan]
    ups = refs[3 * nchan : 4 * nchan]
    filters = refs[4 * nchan]
    outs = refs[4 * nchan + 1 : 5 * nchan + 1]
    delta = refs[5 * nchan + 1]
    planes, upstream, activated = refs[5 * nchan + 2 :]
    part = lax.axis_index("chan")
    share = own[0].shape[1]
    full = nchan * share
    gather_planes(nchan, planes, own, None, sib, pair)
    for k in range(nchan):
        upstream[:, lax.rem(part + nchan - k, nchan)] = ups[k][0 : rows + 2]
    extra = ones_rows(128)
    w = filters[...]
    for g in range((rows + 2) // 2):
        rhs = jnp.concatenate(
            [taps_of(planes, 2 * g, extra), taps_of(planes, 2 * g + 1, extra)], axis=1
        )
        y = jnp.dot(w, rhs, preferred_element_type=f32)
        for n in range(2):
            r = 2 * g + n
            v = shift_sum(y[:, n * 128 : (n + 1) * 128], full)
            e = jnp.exp(-jnp.abs(v))
            inv = 1.0 / (1.0 + e)
            sig = jnp.where(v >= 0, 1.0, e) * inv
            u = upstream[r].reshape(full, 128).astype(f32)
            delta[r] = (u * (leakage + (1.0 - leakage) * sig)).astype(bf16)
            if 1 <= r <= rows:
                soft = jnp.maximum(v, 0.0) + jnp.log(1.0 + e)
                act = (leakage * v + (1.0 - leakage) * soft).astype(bf16)
                activated[r - 1] = act.reshape(nchan, share, 128)
    for k in range(nchan):
        outs[k][...] = activated[:, lax.rem(part + k, nchan)]


def wgrad_body(nchan, rows, step, *refs):
    own, sib, pair = refs[:nchan], refs[nchan : 2 * nchan], refs[2 * nchan : 3 * nchan]
    delta = refs[3 * nchan]
    kept, sent, planes, acc = refs[3 * nchan + 1 :]
    part = lax.axis_index("chan")
    share = own[0].shape[1]
    full = nchan * share
    gather_planes(nchan, planes, own, None, sib, pair)
    extra = ones_rows(128)
    lane = lax.broadcasted_iota(jnp.int32, (full, 128), 1)
    total = None
    for g in range(rows // step):
        lhs, rhs = [], []
        for r in range(g * step + 1, (g + 1) * step + 1):
            d = delta[r].astype(f32)
            before = jnp.where(lane == 127, 0.0, pltpu.roll(d, 127, 1))
            after = jnp.where(lane == 0, 0.0, pltpu.roll(d, 1, 1))
            lhs.append(
                jnp.concatenate([before.astype(bf16), delta[r], after.astype(bf16)], axis=0)
            )
            rhs.append(taps_of(planes, r, extra))
        term = lax.dot_general(
            jnp.concatenate(lhs, axis=1),
            jnp.concatenate(rhs, axis=1),
            (((1,), (1,)), ((), ())),
            preferred_element_type=f32,
        )
        total = term if total is None else total + term
    for c in range(3):
        for q in range(nchan):
            at = (q * 3 + c) * share
            acc[at : at + share] = total[c * full + q * share : c * full + (q + 1) * share]
    half = 3 * share // 2
    for k in range(nchan):
        at = lax.rem(part + k, nchan) * 3 * share
        kept[k] = acc[pl.ds(pl.multiple_of(at + core() * half, 8), half)]
        sent[k] = acc[pl.ds(pl.multiple_of(at + (1 - core()) * half, 8), half)].astype(bf16)


def backward_body(nchan, rows, *refs):
    own, sib, pair, filters = refs[:4]
    outs = refs[4 : 4 + nchan]
    planes, result = refs[4 + nchan :]
    part = lax.axis_index("chan")
    share = outs[0].shape[1]
    full = nchan * share
    even = lax.rem(lax.axis_index("space"), 2) == 0
    planes[:, 1] = own[...]
    planes[:, jnp.where(even, 2, 0)] = sib[...]
    at_pair = jnp.where(even, 0, 2)
    planes[:, at_pair] = pair[...]

    @pl.when(outermost())
    def _():
        planes[:, at_pair] = jnp.zeros(pair.shape, bf16)

    extra = jnp.zeros((64, 128), bf16)
    w = filters[...]
    for g in range(rows // 2):
        rhs = jnp.concatenate(
            [taps_of(planes, 2 * g, extra), taps_of(planes, 2 * g + 1, extra)], axis=1
        )
        y = jnp.dot(w, rhs, preferred_element_type=f32)
        for n in range(2):
            v = shift_sum(y[:, n * 128 : (n + 1) * 128], full)
            result[2 * g + n] = v.astype(bf16).reshape(nchan, share, 128)
    for k in range(nchan):
        outs[k][...] = result[:, lax.rem(part + k, nchan)]


def unpack_body(nchan, rows, height, *refs):
    blocks = refs[:nchan]
    out, flat = refs[nchan:]
    share = out.shape[0]
    part = lax.axis_index("chan")
    size = rows * share
    for k in range(nchan):
        q = lax.rem(part + nchan - k, nchan)
        flat[pl.ds(pl.multiple_of(q * size, 8), size)] = (
            blocks[k][...].astype(f32).reshape(size, 128)
        )
    for ch in range(share):
        out[ch] = flat[pl.ds(ch, height, stride=share)].astype(bf16)


def finish_body(share, factor, mine, other, out, bias, both):
    half = 3 * share // 2
    both[pl.ds(pl.multiple_of(core() * half, 8), half)] = mine[...]
    both[pl.ds(pl.multiple_of((1 - core()) * half, 8), half)] = other[...]
    total = both[...] * factor
    for a in range(3):
        for b in range(3):
            for c in range(3):
                t = b * 3 + a
                out[tap(a, b, c)] = total[c * share : (c + 1) * share, t * 64 : t * 64 + 64]
    col = total[share : 2 * share, 576:577]
    eye = lax.broadcasted_iota(jnp.int32, (share, share), 0) == lax.broadcasted_iota(
        jnp.int32, (share, share), 1
    )
    bias[...] = jnp.sum(jnp.where(eye, col, 0.0), axis=0, keepdims=True)


def kept_sum(first, others):
    total = first.astype(f32)
    for term in others:
        total = total + term.astype(f32)
    return total


def shards(volume, weight, bias, upstream):
    nchan, nspace = lax.axis_size("chan"), lax.axis_size("space")
    share, depth, height, width = volume.shape
    assert depth == 1 and width == 128 and height % nchan == 0
    full = nchan * share
    rows = height // nchan
    factor = 1.0 / math.sqrt(nspace * depth * height * width)
    sib_perm = [(i, i ^ 1) for i in range(nspace)]
    pairs = [(i, i + 1) for i in range(1, nspace - 1, 2)]
    pairs += [(j, i) for i, j in pairs]
    pair_perm = [(i * nchan + c, j * nchan + c) for i, j in pairs for c in range(nchan)]
    ends = (0, nspace - 1)
    turn_perm = [
        (i * nchan + c, i * nchan + (c + 1) % nchan) for i in ends for c in range(nchan)
    ]
    wrap_perm = [
        (i * nchan + c, (nspace - 1 - i) * nchan + c) for i in ends for c in range(nchan)
    ]

    def over_chan(blocks):
        got = []
        for k in range(1, nchan):
            perm = [(i, (i + k) % nchan) for i in range(nchan)]
            got.append(lax.ppermute(blocks[k - 1], "chan", perm))
        return got

    def to_sib(x):
        return lax.ppermute(x, "space", sib_perm)

    def to_pair(x, wrap):
        perm = pair_perm + (wrap_perm if wrap else turn_perm)
        return lax.ppermute(x, ("space", "chan"), perm)

    slabs = jnp.transpose(weight, (2, 3, 4, 0, 1)).reshape(27, share, full)
    block = share * height * width * 2
    v_shape = shape(rows + 4, share, 128)
    u_shape = shape(rows + 17, share, 128)
    v_own, *v_out = call(
        functools.partial(pack_volume_body, nchan, rows),
        [v_shape] * nchan,
        [
            pltpu.VMEM((share * height, width), f32),
            pltpu.VMEM((height + 4, share, width), bf16),
        ],
        0,
        2 * block,
        name="pack_volume",
    )(volume.reshape(share, height, width))
    v_got = over_chan(v_out)
    own_sib, own_pair = to_sib(v_own), to_pair(v_own, VWRAP)
    u_own, *u_out = call(
        functools.partial(pack_rest_body, nchan, rows),
        [u_shape] * nchan,
        [
            pltpu.VMEM((share * height, width), f32),
            pltpu.VMEM((height + 2, share, width), bf16),
        ],
        0,
        3 * block,
        name="pack_rest",
    )(upstream.reshape(share, height, width), slabs, bias.reshape(1, share))
    if UBAR:
        u_out, v_got = lax.optimization_barrier((u_out, v_got))
    v_got, own_sib, own_pair = lax.optimization_barrier((v_got, own_sib, own_pair))
    mine = [v_own] + v_got
    sib = [own_sib] + [to_sib(x) for x in v_got]
    pair = [own_pair] + [to_pair(x, VWRAP2) for x in v_got]
    u_got = over_chan(u_out)
    w_forward, w_backward = call(
        functools.partial(filters_body, nchan, rows),
        [shape(3 * full, 640), shape(3 * full, 640)],
        [pltpu.VMEM((nchan, 15, share, 128), bf16), pltpu.VMEM((640, 256), f32)],
        0,
        1 << 20,
        name="filters",
    )(u_own, *u_got)
    planes = pltpu.VMEM((rows + 4, 3, nchan, share, 128), bf16)
    cells = rows * width
    a_shape = shape(rows, share, 128)
    *act, delta = call(
        functools.partial(forward_body, nchan, rows),
        [a_shape] * nchan + [shape(rows + 2, full, 128)],
        [
            planes,
            pltpu.VMEM((rows + 2, nchan, share, 128), bf16),
            pltpu.VMEM((rows, nchan, share, 128), bf16),
        ],
        2 * 27 * full * full * cells,
        6 * block,
        2 * full * cells,
        name="forward",
    )(*mine, *sib, *pair, u_own, *u_got, w_forward)
    d_sib, d_pair = to_sib(delta), to_pair(delta, DWRAP)
    step = 4 if rows % 4 == 0 else 1
    h_shape = (nchan, 3 * share // 2, 640)
    kept, sent = call(
        functools.partial(wgrad_body, nchan, rows, step),
        [shape(*h_shape, dtype=f32), shape(*h_shape)],
        [planes, pltpu.VMEM((3 * full, 640), f32)],
        2 * 27 * full * full * cells,
        6 * block,
        name="wgrad",
    )(*mine, *sib, *pair, delta)
    kept = kept + to_sib(sent).astype(f32)
    sent = [kept[k].astype(bf16) for k in range(nchan)]
    near = kept_sum(sent[0], over_chan(sent[1:]))
    far = [
        lax.ppermute(
            sent[k],
            ("space", "chan"),
            [
                (i * nchan + c, (i ^ 2 * ZHOP) * nchan + (c + k) % nchan)
                for i in range(nspace)
                for c in range(nchan)
            ],
        )
        for k in range(nchan)
    ]
    total = near + kept_sum(far[0], far[1:])
    def unpack(blocks, name):
        out = call(
            functools.partial(unpack_body, nchan, rows, height),
            shape(share, height, width),
            [pltpu.VMEM((height * share, 128), f32)],
            0,
            2 * block,
            name=name,
        )(*blocks)
        return out.reshape(share, 1, height, width)

    activated = unpack([act[0]] + over_chan(act[1:]), "unpack_activated")
    ig = call(
        functools.partial(backward_body, nchan, rows),
        [a_shape] * nchan,
        [
            pltpu.VMEM((rows + 2, 3, full, 128), bf16),
            pltpu.VMEM((rows, nchan, share, 128), bf16),
        ],
        2 * 27 * full * full * cells,
        6 * block,
        name="backward",
    )(delta, d_sib, d_pair, w_backward)
    ig_got = over_chan(ig[1:])
    hops = [1 << n for n in range(1, nspace.bit_length() - 1)]
    hops.remove(2 * ZHOP)
    if FLIP:
        hops = hops[1:] + hops[:1]
    for n, hop in enumerate(hops):
        if n == DBAR:
            total, d_sib, d_pair = lax.optimization_barrier((total, d_sib, d_pair))
        if n == IBAR:
            total, ig = lax.optimization_barrier((total, ig))
        if n == GBAR:
            total, ig_got = lax.optimization_barrier((total, ig_got))
        if n == ABAR:
            total, activated = lax.optimization_barrier((total, activated))
        sent = total.astype(bf16)
        came = lax.ppermute(sent, "space", [(i, i ^ hop) for i in range(nspace)])
        total = sent.astype(f32) + came.astype(f32)
    if SBAR:
        total, ig_got = lax.optimization_barrier((total, ig_got))
    summed = to_sib(total)

    input_grad = unpack([ig[0]] + ig_got, "unpack_input_grad")
    w_grad, b_grad = call(
        functools.partial(finish_body, share, factor),
        [shape(27, share, full, dtype=f32), shape(1, share, dtype=f32)],
        [pltpu.VMEM((3 * share, 640), f32)],
        0,
        1 << 20,
        name="finish",
    )(total, summed)
    w_grad = jnp.transpose(w_grad.reshape(3, 3, 3, share, full), (3, 4, 0, 1, 2))
    return activated, input_grad, w_grad, b_grad.reshape(share)


def solution(mesh):
    placed = (
        P("chan", "space", None, None),
        P("chan", None, None, None, None),
        P("chan"),
        P("chan", "space", None, None),
    )
    return jax.shard_map(
        shards,
        mesh=mesh,
        in_specs=placed,
        out_specs=(
            P("chan", "space", None, None),
            P("chan", "space", None, None),
            P("chan", None, None, None, None),
            P("chan"),
        ),
        check_vma=False,
    )
```

```python
import functools
import math

import jax
import jax.numpy as jnp
from jax import lax
from jax.experimental import pallas as pl
from jax.experimental.pallas import tpu as pltpu
from jax.sharding import PartitionSpec as P

leakage = 0.1
bf16 = jnp.bfloat16
f32 = jnp.float32
LIMIT = 48 * 1024 * 1024


def call(body, out_shape, scratch, flops, nbytes, trans=0, name=None, **specs):
    return pl.pallas_call(
        body,
        out_shape=out_shape,
        **specs,
        scratch_shapes=scratch,
        compiler_params=pltpu.CompilerParams(vmem_limit_bytes=LIMIT),
        cost_estimate=pl.CostEstimate(
            flops=flops, bytes_accessed=nbytes, transcendentals=trans
        ),
        name=name,
    )


def shape(*dims, dtype=bf16):
    return jax.ShapeDtypeStruct(dims, dtype)


def tap(a, b, c):
    return (a * 3 + b) * 3 + c


def rows_first(src, flat, dst, rim):
    share, height, _ = src.shape
    zero = jnp.zeros((rim, share, 128), bf16)
    flat[...] = src[...].astype(f32).reshape(share * height, 128)
    dst[0:rim] = zero
    dst[height + rim : height + 2 * rim] = zero
    for h in range(height):
        dst[h + rim] = flat[pl.ds(h, share, stride=height)].astype(bf16)


def pack_volume_body(nchan, rows, *refs):
    vol = refs[0]
    outs = refs[1 : 1 + nchan]
    flat, vt = refs[1 + nchan :]
    part = lax.axis_index("chan")
    rows_first(vol, flat, vt, 2)
    for k in range(nchan):
        outs[k][...] = vt[pl.ds(lax.rem(part + k, nchan) * rows, rows + 4)]


def core():
    return lax.rem(lax.axis_index("space"), 2)


def pack_rest_body(nchan, rows, *refs):
    up, w, bias = refs[:3]
    outs = refs[3 : 3 + nchan]
    flat, ut = refs[3 + nchan :]
    share = up.shape[0]
    part = lax.axis_index("chan")
    rows_first(up, flat, ut, 1)
    lane = lax.broadcasted_iota(jnp.int32, (share, 64), 1)
    row = lax.broadcasted_iota(jnp.int32, (share, share), 0)
    col = lax.broadcasted_iota(jnp.int32, (share, share), 1)
    b = jnp.sum(jnp.where(row == col, bias[...], 0.0), axis=1, keepdims=True)
    b0 = b.astype(bf16).astype(f32)
    b1 = (b - b0).astype(bf16).astype(f32)
    b2 = b - b0 - b1
    pieces = jnp.where(
        lane == 0, b0, jnp.where(lane == 1, b1, jnp.where(lane == 2, b2, 0.0))
    )
    none = jnp.zeros((share, 64), f32)
    for c in range(3):
        for j in range(5):
            halves = []
            for t in (2 * j, 2 * j + 1):
                if t < 9:
                    halves.append(w[tap(t % 3, t // 3, c)].astype(f32))
                else:
                    halves.append(pieces if c == 1 else none)
            value = jnp.concatenate(halves, axis=1).astype(bf16)
            for k in range(nchan):
                outs[k][rows + 2 + c * 5 + j] = value
    for k in range(nchan):
        outs[k][0 : rows + 2] = ut[pl.ds(lax.rem(part + k, nchan) * rows, rows + 2)]


def filters_body(nchan, rows, *refs):
    blocks = refs[:nchan]
    forward, backward, wall, turned = refs[nchan:]
    share = blocks[0].shape[1]
    part = lax.axis_index("chan")
    for k in range(nchan):
        wall[lax.rem(part + nchan - k, nchan)] = blocks[k][rows + 2 :]
    full = nchan * share
    for c in range(3):
        for j in range(5):
            block = wall[:, c * 5 + j].reshape(full, 128)
            forward[c * full : (c + 1) * full, j * 128 : (j + 1) * 128] = block
    turned[...] = jnp.zeros_like(turned)
    for b in range(3):
        for a in range(3):
            s = b * 3 + a
            t = (2 - b) * 3 + (2 - a)
            for c in range(3):
                block = wall[:, (2 - c) * 5 + t // 2].reshape(full, 128).astype(f32)
                half = block[:, (t % 2) * 64 : (t % 2) * 64 + 64]
                turned[s * 64 : (s + 1) * 64, c * 64 : (c + 1) * 64] = half
    backward[...] = turned[...].T[: 3 * 64].astype(bf16)


def outermost():
    at = lax.axis_index("space")
    return (at == 0) | (at == lax.axis_size("space") - 1)


def gather_planes(nchan, planes, own, mine, sib, pair):
    part = lax.axis_index("chan")
    even = lax.rem(lax.axis_index("space"), 2) == 0
    at_sib = jnp.where(even, 2, 0)
    at_pair = jnp.where(even, 0, 2)
    for place, blocks in ((1, own), (at_sib, sib), (at_pair, pair)):
        for k in range(nchan):
            planes[:, place, lax.rem(part + nchan - k, nchan)] = blocks[k][...]

    @pl.when(outermost())
    def _():
        planes[:, at_pair] = jnp.zeros(planes[:, at_pair].shape, bf16)


def ones_rows(width):
    row = lax.broadcasted_iota(jnp.int32, (64, width), 0)
    return jnp.where(row < 3, 1.0, 0.0).astype(bf16)


def taps_of(planes, r, extra):
    block = planes[r : r + 3].reshape(-1, 128)
    return jnp.concatenate([block, extra], axis=0)


def shift_sum(y, full):
    lane = lax.broadcasted_iota(jnp.int32, (full, 128), 1)
    left = jnp.where(lane == 0, 0.0, pltpu.roll(y[:full], 1, 1))
    right = jnp.where(lane == 127, 0.0, pltpu.roll(y[2 * full :], 127, 1))
    return y[full : 2 * full] + left + right


def forward_body(nchan, rows, step, *refs):
    own, sib, pair = refs[:nchan], refs[nchan : 2 * nchan], refs[2 * nchan : 3 * nchan]
    ups = refs[3 * nchan : 4 * nchan]
    filters = refs[4 * nchan]
    outs = refs[4 * nchan + 1 : 5 * nchan + 1]
    delta, kept, sent, planes, upstream, activated, acc = refs[5 * nchan + 1 :]
    part = lax.axis_index("chan")
    share = own[0].shape[1]
    full = nchan * share
    gather_planes(nchan, planes, own, None, sib, pair)
    for k in range(nchan):
        upstream[:, lax.rem(part + nchan - k, nchan)] = ups[k][0 : rows + 2]
    extra = ones_rows(128)
    w = filters[...]
    for g in range((rows + 2) // 2):
        rhs = jnp.concatenate(
            [taps_of(planes, 2 * g, extra), taps_of(planes, 2 * g + 1, extra)], axis=1
        )
        y = jnp.dot(w, rhs, preferred_element_type=f32)
        for n in range(2):
            r = 2 * g + n
            v = shift_sum(y[:, n * 128 : (n + 1) * 128], full)
            e = jnp.exp(-jnp.abs(v))
            inv = 1.0 / (1.0 + e)
            sig = jnp.where(v >= 0, 1.0, e) * inv
            u = upstream[r].reshape(full, 128).astype(f32)
            delta[r] = (u * (leakage + (1.0 - leakage) * sig)).astype(bf16)
            if 1 <= r <= rows:
                soft = jnp.maximum(v, 0.0) + jnp.log(1.0 + e)
                act = (leakage * v + (1.0 - leakage) * soft).astype(bf16)
                activated[r - 1] = act.reshape(nchan, share, 128)
    for k in range(nchan):
        outs[k][...] = activated[:, lax.rem(part + k, nchan)]
    lane = lax.broadcasted_iota(jnp.int32, (full, 128), 1)
    total = None
    for g in range(rows // step):
        lhs, rhs = [], []
        for r in range(g * step + 1, (g + 1) * step + 1):
            d = delta[r].astype(f32)
            before = jnp.where(lane == 127, 0.0, pltpu.roll(d, 127, 1))
            after = jnp.where(lane == 0, 0.0, pltpu.roll(d, 1, 1))
            lhs.append(
                jnp.concatenate([before.astype(bf16), delta[r], after.astype(bf16)], axis=0)
            )
            rhs.append(taps_of(planes, r, extra))
        term = lax.dot_general(
            jnp.concatenate(lhs, axis=1),
            jnp.concatenate(rhs, axis=1),
            (((1,), (1,)), ((), ())),
            preferred_element_type=f32,
        )
        total = term if total is None else total + term
    for c in range(3):
        for q in range(nchan):
            at = (q * 3 + c) * share
            acc[at : at + share] = total[c * full + q * share : c * full + (q + 1) * share]
    half = 3 * share // 2
    for k in range(nchan):
        at = lax.rem(part + k, nchan) * 3 * share
        kept[k] = acc[pl.ds(pl.multiple_of(at + core() * half, 8), half)]
        sent[k] = acc[pl.ds(pl.multiple_of(at + (1 - core()) * half, 8), half)].astype(bf16)


def backward_body(nchan, rows, *refs):
    own, sib, pair, filters = refs[:4]
    outs = refs[4 : 4 + nchan]
    planes, result = refs[4 + nchan :]
    part = lax.axis_index("chan")
    share = outs[0].shape[1]
    full = nchan * share
    even = lax.rem(lax.axis_index("space"), 2) == 0
    planes[:, 1] = own[...]
    planes[:, jnp.where(even, 2, 0)] = sib[...]
    at_pair = jnp.where(even, 0, 2)
    planes[:, at_pair] = pair[...]

    @pl.when(outermost())
    def _():
        planes[:, at_pair] = jnp.zeros(pair.shape, bf16)

    extra = jnp.zeros((64, 128), bf16)
    w = filters[...]
    for g in range(rows // 2):
        rhs = jnp.concatenate(
            [taps_of(planes, 2 * g, extra), taps_of(planes, 2 * g + 1, extra)], axis=1
        )
        y = jnp.dot(w, rhs, preferred_element_type=f32)
        for n in range(2):
            v = shift_sum(y[:, n * 128 : (n + 1) * 128], full)
            result[2 * g + n] = v.astype(bf16).reshape(nchan, share, 128)
    for k in range(nchan):
        outs[k][...] = result[:, lax.rem(part + k, nchan)]


def unpack_body(nchan, rows, height, *refs):
    blocks = refs[:nchan]
    out, staged, flat, sems = refs[nchan:]
    share = out.shape[0]
    part = lax.axis_index("chan")
    size = rows * share
    for k in range(nchan):
        q = lax.rem(part + nchan - k, nchan)
        flat[pl.ds(pl.multiple_of(q * size, 8), size)] = (
            blocks[k][...].astype(f32).reshape(size, 128)
        )
    copies = []
    for n in range(4):
        group = pl.ds(n * (share // 4), share // 4)
        for ch in range(n * (share // 4), (n + 1) * (share // 4)):
            staged[ch] = flat[pl.ds(ch, height, stride=share)].astype(bf16)
        copies.append(pltpu.make_async_copy(staged.at[group], out.at[group], sems.at[n]))
        copies[-1].start()
    for copy in copies:
        copy.wait()


def finish_body(share, factor, mine, other, out, bias, both):
    half = 3 * share // 2
    both[pl.ds(pl.multiple_of(core() * half, 8), half)] = mine[...]
    both[pl.ds(pl.multiple_of((1 - core()) * half, 8), half)] = other[...]
    total = both[...] * factor
    for a in range(3):
        for b in range(3):
            for c in range(3):
                t = b * 3 + a
                out[tap(a, b, c)] = total[c * share : (c + 1) * share, t * 64 : t * 64 + 64]
    col = total[share : 2 * share, 576:577]
    eye = lax.broadcasted_iota(jnp.int32, (share, share), 0) == lax.broadcasted_iota(
        jnp.int32, (share, share), 1
    )
    bias[...] = jnp.sum(jnp.where(eye, col, 0.0), axis=0, keepdims=True)


def kept_sum(first, others):
    total = first.astype(f32)
    for term in others:
        total = total + term.astype(f32)
    return total


def shards(volume, weight, bias, upstream):
    nchan, nspace = lax.axis_size("chan"), lax.axis_size("space")
    share, depth, height, width = volume.shape
    assert depth == 1 and width == 128 and height % nchan == 0
    full = nchan * share
    rows = height // nchan
    factor = 1.0 / math.sqrt(nspace * depth * height * width)
    sib_perm = [(i, i ^ 1) for i in range(nspace)]
    pairs = [(i, i + 1) for i in range(1, nspace - 1, 2)]
    pairs += [(j, i) for i, j in pairs]
    pair_perm = [(i * nchan + c, j * nchan + c) for i, j in pairs for c in range(nchan)]
    ends = (0, nspace - 1)
    turn_perm = [
        (i * nchan + c, i * nchan + (c + 1) % nchan) for i in ends for c in range(nchan)
    ]
    wrap_perm = [
        (i * nchan + c, (nspace - 1 - i) * nchan + c) for i in ends for c in range(nchan)
    ]

    def over_chan(blocks):
        got = []
        for k in range(1, nchan):
            perm = [(i, (i + k) % nchan) for i in range(nchan)]
            got.append(lax.ppermute(blocks[k - 1], "chan", perm))
        return got

    def to_sib(x):
        return lax.ppermute(x, "space", sib_perm)

    def to_pair(x, wrap):
        perm = pair_perm + (wrap_perm if wrap else turn_perm)
        return lax.ppermute(x, ("space", "chan"), perm)

    slabs = jnp.transpose(weight, (2, 3, 4, 0, 1)).reshape(27, share, full)
    block = share * height * width * 2
    v_shape = shape(rows + 4, share, 128)
    u_shape = shape(rows + 17, share, 128)
    v_own, *v_out = call(
        functools.partial(pack_volume_body, nchan, rows),
        [v_shape] * nchan,
        [
            pltpu.VMEM((share * height, width), f32),
            pltpu.VMEM((height + 4, share, width), bf16),
        ],
        0,
        2 * block,
        name="pack_volume",
    )(volume.reshape(share, height, width))
    v_got = over_chan(v_out)
    own_sib, own_pair = to_sib(v_own), to_pair(v_own, True)
    u_own, *u_out = call(
        functools.partial(pack_rest_body, nchan, rows),
        [u_shape] * nchan,
        [
            pltpu.VMEM((share * height, width), f32),
            pltpu.VMEM((height + 2, share, width), bf16),
        ],
        0,
        3 * block,
        name="pack_rest",
    )(upstream.reshape(share, height, width), slabs, bias.reshape(1, share))
    v_got, own_pair = lax.optimization_barrier((v_got, own_pair))
    mine = [v_own] + v_got
    sib = [own_sib] + [to_sib(x) for x in v_got]
    pair = [own_pair] + [to_pair(x, True) for x in v_got]
    u_got = over_chan(u_out)
    w_forward, w_backward = call(
        functools.partial(filters_body, nchan, rows),
        [shape(3 * full, 640), shape(3 * full, 640)],
        [pltpu.VMEM((nchan, 15, share, 128), bf16), pltpu.VMEM((640, 256), f32)],
        0,
        1 << 20,
        name="filters",
    )(u_own, *u_got)
    planes = pltpu.VMEM((rows + 4, 3, nchan, share, 128), bf16)
    cells = rows * width
    a_shape = shape(rows, share, 128)
    step = 4 if rows % 4 == 0 else 1
    h_shape = (nchan, 3 * share // 2, 640)
    *act, delta, kept, sent = call(
        functools.partial(forward_body, nchan, rows, step),
        [a_shape] * nchan
        + [shape(rows + 2, full, 128), shape(*h_shape, dtype=f32), shape(*h_shape)],
        [
            planes,
            pltpu.VMEM((rows + 2, nchan, share, 128), bf16),
            pltpu.VMEM((rows, nchan, share, 128), bf16),
            pltpu.VMEM((3 * full, 640), f32),
        ],
        4 * 27 * full * full * cells,
        8 * block,
        2 * full * cells,
        name="forward",
    )(*mine, *sib, *pair, u_own, *u_got, w_forward)
    d_sib, d_pair = to_sib(delta), to_pair(delta, False)
    kept = kept + to_sib(sent).astype(f32)
    sent = [kept[k].astype(bf16) for k in range(nchan)]

    def from_hop(blocks, hop):
        got = [
            lax.ppermute(
                blocks[k],
                ("space", "chan"),
                [
                    (i * nchan + c, (i ^ hop) * nchan + (c + k) % nchan)
                    for i in range(nspace)
                    for c in range(nchan)
                ],
            )
            for k in range(len(blocks))
            if hop or k
        ]
        got = got if hop else [blocks[0]] + got
        return kept_sum(got[0], got[1:])

    def from_hops(blocks, hops):
        reach = [0]
        for hop in hops:
            reach += [hop ^ other for other in reach]
        sums = [from_hop(blocks, hop) for hop in reach]
        while len(sums) > 1:
            sums = [a + b for a, b in zip(sums[0::2], sums[1::2])]
        return sums[0]

    near = 4 if nspace > 4 else 2
    total = from_hops(sent, (near,))
    def unpack(blocks, name):
        out = call(
            functools.partial(unpack_body, nchan, rows, height),
            shape(share, height, width),
            [
                pltpu.VMEM((share, height, width), bf16),
                pltpu.VMEM((height * share, 128), f32),
                pltpu.SemaphoreType.DMA((4,)),
            ],
            0,
            2 * block,
            name=name,
            out_specs=pl.BlockSpec(memory_space=pl.ANY),
        )(*blocks)
        return out.reshape(share, 1, height, width)

    activated = unpack([act[0]] + over_chan(act[1:]), "unpack_activated")
    ig = call(
        functools.partial(backward_body, nchan, rows),
        [a_shape] * nchan,
        [
            pltpu.VMEM((rows + 2, 3, full, 128), bf16),
            pltpu.VMEM((rows, nchan, share, 128), bf16),
        ],
        2 * 27 * full * full * cells,
        6 * block,
        name="backward",
    )(delta, d_sib, d_pair, w_backward)
    ig_got = over_chan(ig[1:])
    hops = [1 << n for n in range(1, nspace.bit_length() - 1) if 1 << n != near]
    for hop in hops[1:] + hops[:1]:
        total = from_hops([total.astype(bf16)], (hop,))
    summed = to_sib(total)

    input_grad = unpack([ig[0]] + ig_got, "unpack_input_grad")
    w_grad, b_grad = call(
        functools.partial(finish_body, share, factor),
        [shape(27, share, full, dtype=f32), shape(1, share, dtype=f32)],
        [pltpu.VMEM((3 * share, 640), f32)],
        0,
        1 << 20,
        name="finish",
    )(total, summed)
    w_grad = jnp.transpose(w_grad.reshape(3, 3, 3, share, full), (3, 4, 0, 1, 2))
    return activated, input_grad, w_grad, b_grad.reshape(share)


def solution(mesh):
    placed = (
        P("chan", "space", None, None),
        P("chan", None, None, None, None),
        P("chan"),
        P("chan", "space", None, None),
    )
    return jax.shard_map(
        shards,
        mesh=mesh,
        in_specs=placed,
        out_specs=(
            P("chan", "space", None, None),
            P("chan", "space", None, None),
            P("chan", None, None, None, None),
            P("chan"),
        ),
        check_vma=False,
    )
```

```python
import functools
import math

import jax
import jax.numpy as jnp
from jax import lax
from jax.experimental import pallas as pl
from jax.experimental.pallas import tpu as pltpu
from jax.sharding import PartitionSpec as P

leakage = 0.1
bf16 = jnp.bfloat16
f32 = jnp.float32
LIMIT = 48 * 1024 * 1024


def call(body, out_shape, scratch, flops, nbytes, trans=0, name=None, **specs):
    return pl.pallas_call(
        body,
        out_shape=out_shape,
        **specs,
        scratch_shapes=scratch,
        compiler_params=pltpu.CompilerParams(vmem_limit_bytes=LIMIT),
        cost_estimate=pl.CostEstimate(
            flops=flops, bytes_accessed=nbytes, transcendentals=trans
        ),
        name=name,
    )


def shape(*dims, dtype=bf16):
    return jax.ShapeDtypeStruct(dims, dtype)


def tap(a, b, c):
    return (a * 3 + b) * 3 + c


def rows_first(src, flat, dst, rim):
    share, height, _ = src.shape
    zero = jnp.zeros((rim, share, 128), bf16)
    flat[...] = src[...].astype(f32).reshape(share * height, 128)
    dst[0:rim] = zero
    dst[height + rim : height + 2 * rim] = zero
    for h in range(height):
        dst[h + rim] = flat[pl.ds(h, share, stride=height)].astype(bf16)


def pack_volume_body(nchan, rows, *refs):
    vol = refs[0]
    outs = refs[1 : 1 + nchan]
    flat, vt = refs[1 + nchan :]
    part = lax.axis_index("chan")
    rows_first(vol, flat, vt, 2)
    for k in range(nchan):
        outs[k][...] = vt[pl.ds(lax.rem(part + k, nchan) * rows, rows + 4)]


def core():
    return lax.rem(lax.axis_index("space"), 2)


def pack_rest_body(nchan, rows, *refs):
    up, w, bias = refs[:3]
    outs = refs[3 : 3 + nchan]
    flat, ut = refs[3 + nchan :]
    share = up.shape[0]
    part = lax.axis_index("chan")
    rows_first(up, flat, ut, 1)
    lane = lax.broadcasted_iota(jnp.int32, (share, 64), 1)
    row = lax.broadcasted_iota(jnp.int32, (share, share), 0)
    col = lax.broadcasted_iota(jnp.int32, (share, share), 1)
    b = jnp.sum(jnp.where(row == col, bias[...], 0.0), axis=1, keepdims=True)
    b0 = b.astype(bf16).astype(f32)
    b1 = (b - b0).astype(bf16).astype(f32)
    b2 = b - b0 - b1
    pieces = jnp.where(
        lane == 0, b0, jnp.where(lane == 1, b1, jnp.where(lane == 2, b2, 0.0))
    )
    none = jnp.zeros((share, 64), f32)
    for c in range(3):
        for j in range(5):
            halves = []
            for t in (2 * j, 2 * j + 1):
                if t < 9:
                    halves.append(w[tap(t % 3, t // 3, c)].astype(f32))
                else:
                    halves.append(pieces if c == 1 else none)
            value = jnp.concatenate(halves, axis=1).astype(bf16)
            for k in range(nchan):
                outs[k][rows + 2 + c * 5 + j] = value
    for k in range(nchan):
        outs[k][0 : rows + 2] = ut[pl.ds(lax.rem(part + k, nchan) * rows, rows + 2)]


def gather_filters(nchan, rows, wall, blocks):
    part = lax.axis_index("chan")
    for k in range(nchan):
        wall[lax.rem(part + nchan - k, nchan)] = blocks[k][rows + 2 :]


def backward_filters_body(nchan, rows, *refs):
    blocks = refs[:nchan]
    backward, wall, turned = refs[nchan:]
    full = nchan * blocks[0].shape[1]
    gather_filters(nchan, rows, wall, blocks)
    turned[...] = jnp.zeros_like(turned)
    for a in range(3):
        plane = 0 if a == 1 else 2 - core() if a == 0 else 1 + core()
        for b in range(3):
            at = pl.ds(pl.multiple_of((plane * 3 + b) * 64, 64), 64)
            t = (2 - b) * 3 + (2 - a)
            for c in range(3):
                block = wall[:, (2 - c) * 5 + t // 2].reshape(full, 128).astype(f32)
                half = block[:, (t % 2) * 64 : (t % 2) * 64 + 64]
                turned[at, c * 64 : (c + 1) * 64] = half

    @pl.when(outermost())
    def _():
        turned[6 * 64 : 9 * 64] = jnp.zeros((3 * 64, 256), f32)

    backward[...] = turned[...].T[: 3 * 64].astype(bf16)


def outermost():
    at = lax.axis_index("space")
    return (at == 0) | (at == lax.axis_size("space") - 1)


def gather_planes(nchan, planes, own, mine, sib, pair):
    part = lax.axis_index("chan")
    even = lax.rem(lax.axis_index("space"), 2) == 0
    at_sib = jnp.where(even, 2, 0)
    at_pair = jnp.where(even, 0, 2)
    for place, blocks in ((1, own), (at_sib, sib), (at_pair, pair)):
        for k in range(nchan):
            planes[:, place, lax.rem(part + nchan - k, nchan)] = blocks[k][...]

    @pl.when(outermost())
    def _():
        planes[:, at_pair] = jnp.zeros(planes[:, at_pair].shape, bf16)


def ones_rows(width):
    row = lax.broadcasted_iota(jnp.int32, (64, width), 0)
    return jnp.where(row < 3, 1.0, 0.0).astype(bf16)


def taps_of(planes, r, extra):
    block = planes[r : r + 3].reshape(-1, 128)
    return jnp.concatenate([block, extra], axis=0)


def shift_sum(y, full):
    lane = lax.broadcasted_iota(jnp.int32, (full, 128), 1)
    left = jnp.where(lane == 0, 0.0, pltpu.roll(y[:full], 1, 1))
    right = jnp.where(lane == 127, 0.0, pltpu.roll(y[2 * full :], 127, 1))
    return y[full : 2 * full] + left + right


def forward_body(nchan, rows, step, *refs):
    own, sib, pair = refs[:nchan], refs[nchan : 2 * nchan], refs[2 * nchan : 3 * nchan]
    ups = refs[3 * nchan : 4 * nchan]
    outs = refs[4 * nchan : 5 * nchan]
    delta, kept, sent, planes, upstream, activated, acc, wall, filters = refs[5 * nchan :]
    part = lax.axis_index("chan")
    share = own[0].shape[1]
    full = nchan * share
    gather_planes(nchan, planes, own, None, sib, pair)
    for k in range(nchan):
        upstream[:, lax.rem(part + nchan - k, nchan)] = ups[k][0 : rows + 2]
    gather_filters(nchan, rows, wall, ups)
    for c in range(3):
        for j in range(5):
            block = wall[:, c * 5 + j].reshape(full, 128)
            filters[c * full : (c + 1) * full, j * 128 : (j + 1) * 128] = block
    extra = ones_rows(128)
    w = filters[...]
    for g in range((rows + 2) // 2):
        rhs = jnp.concatenate(
            [taps_of(planes, 2 * g, extra), taps_of(planes, 2 * g + 1, extra)], axis=1
        )
        y = jnp.dot(w, rhs, preferred_element_type=f32)
        for n in range(2):
            r = 2 * g + n
            v = shift_sum(y[:, n * 128 : (n + 1) * 128], full)
            e = jnp.exp(-jnp.abs(v))
            inv = 1.0 / (1.0 + e)
            sig = jnp.where(v >= 0, 1.0, e) * inv
            u = upstream[r].reshape(full, 128).astype(f32)
            delta[r] = (u * (leakage + (1.0 - leakage) * sig)).astype(bf16)
            if 1 <= r <= rows:
                soft = jnp.maximum(v, 0.0) + jnp.log(1.0 + e)
                act = (leakage * v + (1.0 - leakage) * soft).astype(bf16)
                activated[r - 1] = act.reshape(nchan, share, 128)
    for k in range(nchan):
        outs[k][...] = activated[:, lax.rem(part + k, nchan)]
    lane = lax.broadcasted_iota(jnp.int32, (full, 128), 1)
    total = None
    for g in range(rows // step):
        lhs, rhs = [], []
        for r in range(g * step + 1, (g + 1) * step + 1):
            d = delta[r].astype(f32)
            before = jnp.where(lane == 127, 0.0, pltpu.roll(d, 127, 1))
            after = jnp.where(lane == 0, 0.0, pltpu.roll(d, 1, 1))
            lhs.append(
                jnp.concatenate([before.astype(bf16), delta[r], after.astype(bf16)], axis=0)
            )
            rhs.append(taps_of(planes, r, extra))
        term = lax.dot_general(
            jnp.concatenate(lhs, axis=1),
            jnp.concatenate(rhs, axis=1),
            (((1,), (1,)), ((), ())),
            preferred_element_type=f32,
        )
        total = term if total is None else total + term
    for c in range(3):
        for q in range(nchan):
            at = (q * 3 + c) * share
            acc[at : at + share] = total[c * full + q * share : c * full + (q + 1) * share]
    half = 3 * share // 2
    for k in range(nchan):
        at = lax.rem(part + k, nchan) * 3 * share
        kept[k] = acc[pl.ds(pl.multiple_of(at + core() * half, 8), half)]
        sent[k] = acc[pl.ds(pl.multiple_of(at + (1 - core()) * half, 8), half)].astype(bf16)


def backward_body(nchan, rows, *refs):
    sources, filters = refs[:3], refs[3]
    outs = refs[4 : 4 + nchan]
    result = refs[4 + nchan]
    part = lax.axis_index("chan")
    share = outs[0].shape[1]
    full = nchan * share
    extra = jnp.zeros((64, 128), bf16)

    def taps(r):
        blocks = [source[r : r + 3].reshape(-1, 128) for source in sources]
        return jnp.concatenate(blocks + [extra], axis=0)

    w = filters[...]
    for g in range(rows // 2):
        rhs = jnp.concatenate(
            [taps(2 * g), taps(2 * g + 1)], axis=1
        )
        y = jnp.dot(w, rhs, preferred_element_type=f32)
        for n in range(2):
            v = shift_sum(y[:, n * 128 : (n + 1) * 128], full)
            result[2 * g + n] = v.astype(bf16).reshape(nchan, share, 128)
    for k in range(nchan):
        outs[k][...] = result[:, lax.rem(part + k, nchan)]


def unpack_body(nchan, rows, height, *refs):
    blocks = refs[:nchan]
    out, staged, flat, sems = refs[nchan:]
    share = out.shape[0]
    part = lax.axis_index("chan")
    size = rows * share
    for k in range(nchan):
        q = lax.rem(part + nchan - k, nchan)
        flat[pl.ds(pl.multiple_of(q * size, 8), size)] = (
            blocks[k][...].astype(f32).reshape(size, 128)
        )
    copies = []
    for n in range(4):
        group = pl.ds(n * (share // 4), share // 4)
        for ch in range(n * (share // 4), (n + 1) * (share // 4)):
            staged[ch] = flat[pl.ds(ch, height, stride=share)].astype(bf16)
        copies.append(pltpu.make_async_copy(staged.at[group], out.at[group], sems.at[n]))
        copies[-1].start()
    for copy in copies:
        copy.wait()


def finish_body(share, factor, mine, other, out, bias, both):
    half = 3 * share // 2
    both[pl.ds(pl.multiple_of(core() * half, 8), half)] = mine[...]
    both[pl.ds(pl.multiple_of((1 - core()) * half, 8), half)] = other[...]
    total = both[...] * factor
    for a in range(3):
        for b in range(3):
            for c in range(3):
                t = b * 3 + a
                out[tap(a, b, c)] = total[c * share : (c + 1) * share, t * 64 : t * 64 + 64]
    col = total[share : 2 * share, 576:577]
    eye = lax.broadcasted_iota(jnp.int32, (share, share), 0) == lax.broadcasted_iota(
        jnp.int32, (share, share), 1
    )
    bias[...] = jnp.sum(jnp.where(eye, col, 0.0), axis=0, keepdims=True)


def kept_sum(first, others):
    total = first.astype(f32)
    for term in others:
        total = total + term.astype(f32)
    return total


def shards(volume, weight, bias, upstream):
    nchan, nspace = lax.axis_size("chan"), lax.axis_size("space")
    share, depth, height, width = volume.shape
    assert depth == 1 and width == 128 and height % nchan == 0
    full = nchan * share
    rows = height // nchan
    factor = 1.0 / math.sqrt(nspace * depth * height * width)
    sib_perm = [(i, i ^ 1) for i in range(nspace)]
    pairs = [(i, i + 1) for i in range(1, nspace - 1, 2)]
    pairs += [(j, i) for i, j in pairs]
    pair_perm = [(i * nchan + c, j * nchan + c) for i, j in pairs for c in range(nchan)]
    ends = (0, nspace - 1)
    turn_perm = [
        (i * nchan + c, i * nchan + (c + 1) % nchan) for i in ends for c in range(nchan)
    ]
    wrap_perm = [
        (i * nchan + c, (nspace - 1 - i) * nchan + c) for i in ends for c in range(nchan)
    ]

    def over_chan(blocks):
        got = []
        for k in range(1, nchan):
            perm = [(i, (i + k) % nchan) for i in range(nchan)]
            got.append(lax.ppermute(blocks[k - 1], "chan", perm))
        return got

    def to_sib(x):
        return lax.ppermute(x, "space", sib_perm)

    def to_pair(x, wrap):
        perm = pair_perm + (wrap_perm if wrap else turn_perm)
        return lax.ppermute(x, ("space", "chan"), perm)

    slabs = jnp.transpose(weight, (2, 3, 4, 0, 1)).reshape(27, share, full)
    block = share * height * width * 2
    v_shape = shape(rows + 4, share, 128)
    u_shape = shape(rows + 17, share, 128)
    v_own, *v_out = call(
        functools.partial(pack_volume_body, nchan, rows),
        [v_shape] * nchan,
        [
            pltpu.VMEM((share * height, width), f32),
            pltpu.VMEM((height + 4, share, width), bf16),
        ],
        0,
        2 * block,
        name="pack_volume",
    )(volume.reshape(share, height, width))
    v_got = over_chan(v_out)
    own_sib, own_pair = to_sib(v_own), to_pair(v_own, True)
    u_own, *u_out = call(
        functools.partial(pack_rest_body, nchan, rows),
        [u_shape] * nchan,
        [
            pltpu.VMEM((share * height, width), f32),
            pltpu.VMEM((height + 2, share, width), bf16),
        ],
        0,
        3 * block,
        name="pack_rest",
    )(upstream.reshape(share, height, width), slabs, bias.reshape(1, share))
    v_got, own_pair = lax.optimization_barrier((v_got, own_pair))
    mine = [v_own] + v_got
    sib = [own_sib] + [to_sib(x) for x in v_got]
    pair = [own_pair] + [to_pair(x, True) for x in v_got]
    u_got = over_chan(u_out)
    w_backward = call(
        functools.partial(backward_filters_body, nchan, rows),
        shape(3 * full, 640),
        [pltpu.VMEM((nchan, 15, share, 128), bf16), pltpu.VMEM((640, 256), f32)],
        0,
        1 << 20,
        name="filters",
    )(u_own, *u_got)
    planes = pltpu.VMEM((rows + 4, 3, nchan, share, 128), bf16)
    cells = rows * width
    a_shape = shape(rows, share, 128)
    step = 4 if rows % 4 == 0 else 1
    h_shape = (nchan, 3 * share // 2, 640)
    *act, delta, kept, sent = call(
        functools.partial(forward_body, nchan, rows, step),
        [a_shape] * nchan
        + [shape(rows + 2, full, 128), shape(*h_shape, dtype=f32), shape(*h_shape)],
        [
            planes,
            pltpu.VMEM((rows + 2, nchan, share, 128), bf16),
            pltpu.VMEM((rows, nchan, share, 128), bf16),
            pltpu.VMEM((3 * full, 640), f32),
            pltpu.VMEM((nchan, 15, share, 128), bf16),
            pltpu.VMEM((3 * full, 640), bf16),
        ],
        4 * 27 * full * full * cells,
        8 * block,
        2 * full * cells,
        name="forward",
    )(*mine, *sib, *pair, u_own, *u_got)
    d_sib, d_pair = to_sib(delta), to_pair(delta, False)
    kept = kept + to_sib(sent).astype(f32)
    sent = [kept[k].astype(bf16) for k in range(nchan)]

    def from_hop(blocks, hop):
        got = [
            lax.ppermute(
                blocks[k],
                ("space", "chan"),
                [
                    (i * nchan + c, (i ^ hop) * nchan + (c + k) % nchan)
                    for i in range(nspace)
                    for c in range(nchan)
                ],
            )
            for k in range(len(blocks))
            if hop or k
        ]
        got = got if hop else [blocks[0]] + got
        return kept_sum(got[0], got[1:])

    def from_hops(blocks, hops):
        reach = [0]
        for hop in hops:
            reach += [hop ^ other for other in reach]
        sums = [from_hop(blocks, hop) for hop in reach]
        while len(sums) > 1:
            sums = [a + b for a, b in zip(sums[0::2], sums[1::2])]
        return sums[0]

    near = 4 if nspace > 4 else 2
    total = from_hops(sent, (near,))

    def unpack(blocks, name):
        out = call(
            functools.partial(unpack_body, nchan, rows, height),
            shape(share, height, width),
            [
                pltpu.VMEM((share, height, width), bf16),
                pltpu.VMEM((height * share, 128), f32),
                pltpu.SemaphoreType.DMA((4,)),
            ],
            0,
            2 * block,
            name=name,
            out_specs=pl.BlockSpec(memory_space=pl.ANY),
        )(*blocks)
        return out.reshape(share, 1, height, width)

    activated = unpack([act[0]] + over_chan(act[1:]), "unpack_activated")
    ig = call(
        functools.partial(backward_body, nchan, rows),
        [a_shape] * nchan,
        [pltpu.VMEM((rows, nchan, share, 128), bf16)],
        2 * 27 * full * full * cells,
        6 * block,
        name="backward",
    )(delta, d_sib, d_pair, w_backward)
    ig_got = over_chan(ig[1:])
    hops = [1 << n for n in range(1, nspace.bit_length() - 1) if 1 << n != near]
    for hop in hops[1:] + hops[:1]:
        total = from_hops([total.astype(bf16)], (hop,))
    summed = to_sib(total)

    input_grad = unpack([ig[0]] + ig_got, "unpack_input_grad")
    w_grad, b_grad = call(
        functools.partial(finish_body, share, factor),
        [shape(27, share, full, dtype=f32), shape(1, share, dtype=f32)],
        [pltpu.VMEM((3 * share, 640), f32)],
        0,
        1 << 20,
        name="finish",
    )(total, summed)
    w_grad = jnp.transpose(w_grad.reshape(3, 3, 3, share, full), (3, 4, 0, 1, 2))
    return activated, input_grad, w_grad, b_grad.reshape(share)


def solution(mesh):
    placed = (
        P("chan", "space", None, None),
        P("chan", None, None, None, None),
        P("chan"),
        P("chan", "space", None, None),
    )
    return jax.shard_map(
        shards,
        mesh=mesh,
        in_specs=placed,
        out_specs=(
            P("chan", "space", None, None),
            P("chan", "space", None, None),
            P("chan", None, None, None, None),
            P("chan"),
        ),
        check_vma=False,
    )
```

```python
import functools
import math

import jax
import jax.numpy as jnp
from jax import lax
from jax.experimental import pallas as pl
from jax.experimental.pallas import tpu as pltpu
from jax.sharding import PartitionSpec as P

leakage = 0.1
bf16 = jnp.bfloat16
f32 = jnp.float32
LIMIT = 48 * 1024 * 1024


def call(body, out_shape, scratch, flops, nbytes, trans=0, name=None, **specs):
    return pl.pallas_call(
        body,
        out_shape=out_shape,
        **specs,
        scratch_shapes=scratch,
        compiler_params=pltpu.CompilerParams(vmem_limit_bytes=LIMIT),
        cost_estimate=pl.CostEstimate(
            flops=flops, bytes_accessed=nbytes, transcendentals=trans
        ),
        name=name,
    )


def shape(*dims, dtype=bf16):
    return jax.ShapeDtypeStruct(dims, dtype)


def tap(a, b, c):
    return (a * 3 + b) * 3 + c


def rows_first(src, flat, dst, rim):
    share, height, _ = src.shape
    zero = jnp.zeros((rim, share, 128), bf16)
    flat[...] = src[...].astype(f32).reshape(share * height, 128)
    dst[0:rim] = zero
    dst[height + rim : height + 2 * rim] = zero
    for h in range(height):
        dst[h + rim] = flat[pl.ds(h, share, stride=height)].astype(bf16)


def pack_volume_body(nchan, rows, *refs):
    vol = refs[0]
    outs = refs[1 : 1 + nchan]
    flat, vt = refs[1 + nchan :]
    part = lax.axis_index("chan")
    rows_first(vol, flat, vt, 2)
    for k in range(nchan):
        outs[k][...] = vt[pl.ds(lax.rem(part + k, nchan) * rows, rows + 4)]


def core():
    return lax.rem(lax.axis_index("space"), 2)


def pack_rest_body(nchan, rows, *refs):
    up, w, bias = refs[:3]
    outs = refs[3 : 3 + nchan]
    flat, ut = refs[3 + nchan :]
    share = up.shape[0]
    part = lax.axis_index("chan")
    rows_first(up, flat, ut, 1)
    lane = lax.broadcasted_iota(jnp.int32, (share, 64), 1)
    row = lax.broadcasted_iota(jnp.int32, (share, share), 0)
    col = lax.broadcasted_iota(jnp.int32, (share, share), 1)
    b = jnp.sum(jnp.where(row == col, bias[...], 0.0), axis=1, keepdims=True)
    b0 = b.astype(bf16).astype(f32)
    b1 = (b - b0).astype(bf16).astype(f32)
    b2 = b - b0 - b1
    pieces = jnp.where(
        lane == 0, b0, jnp.where(lane == 1, b1, jnp.where(lane == 2, b2, 0.0))
    )
    none = jnp.zeros((share, 64), f32)
    for c in range(3):
        for j in range(5):
            halves = []
            for t in (2 * j, 2 * j + 1):
                if t < 9:
                    halves.append(w[tap(t % 3, t // 3, c)].astype(f32))
                else:
                    halves.append(pieces if c == 1 else none)
            value = jnp.concatenate(halves, axis=1).astype(bf16)
            for k in range(nchan):
                outs[k][rows + 2 + c * 5 + j] = value
    for k in range(nchan):
        outs[k][0 : rows + 2] = ut[pl.ds(lax.rem(part + k, nchan) * rows, rows + 2)]


def gather_filters(nchan, rows, wall, blocks):
    part = lax.axis_index("chan")
    for k in range(nchan):
        wall[lax.rem(part + nchan - k, nchan)] = blocks[k][rows + 2 :]


def backward_filters_body(nchan, rows, *refs):
    blocks = refs[:nchan]
    backward, wall, turned = refs[nchan:]
    full = nchan * blocks[0].shape[1]
    gather_filters(nchan, rows, wall, blocks)
    turned[...] = jnp.zeros_like(turned)
    for a in range(3):
        plane = 0 if a == 1 else 2 - core() if a == 0 else 1 + core()
        for b in range(3):
            at = pl.ds(pl.multiple_of((plane * 3 + b) * 64, 64), 64)
            t = (2 - b) * 3 + (2 - a)
            for c in range(3):
                block = wall[:, (2 - c) * 5 + t // 2].reshape(full, 128).astype(f32)
                half = block[:, (t % 2) * 64 : (t % 2) * 64 + 64]
                turned[at, c * 64 : (c + 1) * 64] = half

    @pl.when(outermost())
    def _():
        turned[6 * 64 : 9 * 64] = jnp.zeros((3 * 64, 256), f32)

    backward[...] = turned[...].T[: 3 * 64].astype(bf16)


def outermost():
    at = lax.axis_index("space")
    return (at == 0) | (at == lax.axis_size("space") - 1)


def gather_planes(nchan, planes, own, mine, sib, pair):
    part = lax.axis_index("chan")
    even = lax.rem(lax.axis_index("space"), 2) == 0
    at_sib = jnp.where(even, 2, 0)
    at_pair = jnp.where(even, 0, 2)
    for place, blocks in ((1, own), (at_sib, sib), (at_pair, pair)):
        for k in range(nchan):
            planes[:, place, lax.rem(part + nchan - k, nchan)] = blocks[k][...]

    @pl.when(outermost())
    def _():
        planes[:, at_pair] = jnp.zeros(planes[:, at_pair].shape, bf16)


def ones_rows(width):
    row = lax.broadcasted_iota(jnp.int32, (64, width), 0)
    return jnp.where(row < 3, 1.0, 0.0).astype(bf16)


def taps_of(planes, r, extra):
    block = planes[r : r + 3].reshape(-1, 128)
    return jnp.concatenate([block, extra], axis=0)


def shift_sum(y, full):
    lane = lax.broadcasted_iota(jnp.int32, (full, 128), 1)
    left = jnp.where(lane == 0, 0.0, pltpu.roll(y[:full], 1, 1))
    right = jnp.where(lane == 127, 0.0, pltpu.roll(y[2 * full :], 127, 1))
    return y[full : 2 * full] + left + right


def forward_body(nchan, rows, step, *refs):
    own, sib, pair = refs[:nchan], refs[nchan : 2 * nchan], refs[2 * nchan : 3 * nchan]
    ups = refs[3 * nchan : 4 * nchan]
    outs = refs[4 * nchan : 5 * nchan]
    delta, kept, sent, planes, upstream, activated, acc, wall, filters = refs[5 * nchan :]
    part = lax.axis_index("chan")
    share = own[0].shape[1]
    full = nchan * share
    gather_planes(nchan, planes, own, None, sib, pair)
    for k in range(nchan):
        upstream[:, lax.rem(part + nchan - k, nchan)] = ups[k][0 : rows + 2]
    gather_filters(nchan, rows, wall, ups)
    for c in range(3):
        for j in range(5):
            block = wall[:, c * 5 + j].reshape(full, 128)
            filters[c * full : (c + 1) * full, j * 128 : (j + 1) * 128] = block
    extra = ones_rows(128)
    w = filters[...]
    for g in range((rows + 2) // 2):
        rhs = jnp.concatenate(
            [taps_of(planes, 2 * g, extra), taps_of(planes, 2 * g + 1, extra)], axis=1
        )
        y = jnp.dot(w, rhs, preferred_element_type=f32)
        for n in range(2):
            r = 2 * g + n
            v = shift_sum(y[:, n * 128 : (n + 1) * 128], full)
            e = jnp.exp(-jnp.abs(v))
            inv = 1.0 / (1.0 + e)
            sig = jnp.where(v >= 0, 1.0, e) * inv
            u = upstream[r].reshape(full, 128).astype(f32)
            delta[r] = (u * (leakage + (1.0 - leakage) * sig)).astype(bf16)
            if 1 <= r <= rows:
                soft = jnp.maximum(v, 0.0) + jnp.log(1.0 + e)
                act = (leakage * v + (1.0 - leakage) * soft).astype(bf16)
                activated[r - 1] = act.reshape(nchan, share, 128)
    for k in range(nchan):
        outs[k][...] = activated[:, lax.rem(part + k, nchan)]
    lane = lax.broadcasted_iota(jnp.int32, (full, 128), 1)
    total = None
    for g in range(rows // step):
        lhs, rhs = [], []
        for r in range(g * step + 1, (g + 1) * step + 1):
            d = delta[r].astype(f32)
            before = jnp.where(lane == 127, 0.0, pltpu.roll(d, 127, 1))
            after = jnp.where(lane == 0, 0.0, pltpu.roll(d, 1, 1))
            lhs.append(
                jnp.concatenate([before.astype(bf16), delta[r], after.astype(bf16)], axis=0)
            )
            rhs.append(taps_of(planes, r, extra))
        term = lax.dot_general(
            jnp.concatenate(lhs, axis=1),
            jnp.concatenate(rhs, axis=1),
            (((1,), (1,)), ((), ())),
            preferred_element_type=f32,
        )
        total = term if total is None else total + term
    for c in range(3):
        for q in range(nchan):
            at = (q * 3 + c) * share
            acc[at : at + share] = total[c * full + q * share : c * full + (q + 1) * share]
    half = 3 * share // 2
    for k in range(nchan):
        at = lax.rem(part + k, nchan) * 3 * share
        kept[k] = acc[pl.ds(pl.multiple_of(at + core() * half, 8), half)]
        sent[k] = acc[pl.ds(pl.multiple_of(at + (1 - core()) * half, 8), half)].astype(bf16)


def backward_body(nchan, rows, *refs):
    sources, filters = refs[:3], refs[3]
    outs = refs[4 : 4 + nchan]
    result = refs[4 + nchan]
    part = lax.axis_index("chan")
    share = outs[0].shape[1]
    full = nchan * share
    extra = jnp.zeros((64, 128), bf16)

    def taps(r):
        blocks = [source[r : r + 3].reshape(-1, 128) for source in sources]
        return jnp.concatenate(blocks + [extra], axis=0)

    w = filters[...]
    for g in range(rows // 2):
        rhs = jnp.concatenate(
            [taps(2 * g), taps(2 * g + 1)], axis=1
        )
        y = jnp.dot(w, rhs, preferred_element_type=f32)
        for n in range(2):
            v = shift_sum(y[:, n * 128 : (n + 1) * 128], full)
            result[2 * g + n] = v.astype(bf16).reshape(nchan, share, 128)
    for k in range(nchan):
        outs[k][...] = result[:, lax.rem(part + k, nchan)]


def unpack_body(nchan, rows, height, *refs):
    blocks = refs[:nchan]
    out, staged, flat, sems = refs[nchan:]
    share = out.shape[0]
    part = lax.axis_index("chan")
    pitch = share + 8
    for k in range(nchan):
        q = lax.rem(part + nchan - k, nchan)
        for row in range(rows):
            at = pl.multiple_of(q * (rows * pitch) + row * pitch, 8)
            flat[pl.ds(at, share)] = blocks[k][row].astype(f32)
    copies = []
    for n in range(4):
        group = pl.ds(n * (share // 4), share // 4)
        for ch in range(n * (share // 4), (n + 1) * (share // 4)):
            staged[ch] = flat[pl.ds(ch, height, stride=pitch)].astype(bf16)
        copies.append(pltpu.make_async_copy(staged.at[group], out.at[group], sems.at[n]))
        copies[-1].start()
    for copy in copies:
        copy.wait()


def finish_body(share, factor, mine, other, out, bias, both):
    half = 3 * share // 2
    both[pl.ds(pl.multiple_of(core() * half, 8), half)] = mine[...]
    both[pl.ds(pl.multiple_of((1 - core()) * half, 8), half)] = other[...]
    total = both[...] * factor
    for a in range(3):
        for b in range(3):
            for c in range(3):
                t = b * 3 + a
                out[tap(a, b, c)] = total[c * share : (c + 1) * share, t * 64 : t * 64 + 64]
    col = total[share : 2 * share, 576:577]
    eye = lax.broadcasted_iota(jnp.int32, (share, share), 0) == lax.broadcasted_iota(
        jnp.int32, (share, share), 1
    )
    bias[...] = jnp.sum(jnp.where(eye, col, 0.0), axis=0, keepdims=True)


def kept_sum(first, others):
    total = first.astype(f32)
    for term in others:
        total = total + term.astype(f32)
    return total


def shards(volume, weight, bias, upstream):
    nchan, nspace = lax.axis_size("chan"), lax.axis_size("space")
    share, depth, height, width = volume.shape
    assert depth == 1 and width == 128 and height % nchan == 0
    full = nchan * share
    rows = height // nchan
    factor = 1.0 / math.sqrt(nspace * depth * height * width)
    sib_perm = [(i, i ^ 1) for i in range(nspace)]
    pairs = [(i, i + 1) for i in range(1, nspace - 1, 2)]
    pairs += [(j, i) for i, j in pairs]
    pair_perm = [(i * nchan + c, j * nchan + c) for i, j in pairs for c in range(nchan)]
    ends = (0, nspace - 1)
    turn_perm = [
        (i * nchan + c, i * nchan + (c + 1) % nchan) for i in ends for c in range(nchan)
    ]
    wrap_perm = [
        (i * nchan + c, (nspace - 1 - i) * nchan + c) for i in ends for c in range(nchan)
    ]

    def over_chan(blocks):
        got = []
        for k in range(1, nchan):
            perm = [(i, (i + k) % nchan) for i in range(nchan)]
            got.append(lax.ppermute(blocks[k - 1], "chan", perm))
        return got

    def to_sib(x):
        return lax.ppermute(x, "space", sib_perm)

    def to_pair(x, wrap):
        perm = pair_perm + (wrap_perm if wrap else turn_perm)
        return lax.ppermute(x, ("space", "chan"), perm)

    slabs = jnp.transpose(weight, (2, 3, 4, 0, 1)).reshape(27, share, full)
    block = share * height * width * 2
    v_shape = shape(rows + 4, share, 128)
    u_shape = shape(rows + 17, share, 128)
    v_own, *v_out = call(
        functools.partial(pack_volume_body, nchan, rows),
        [v_shape] * nchan,
        [
            pltpu.VMEM((share * height, width), f32),
            pltpu.VMEM((height + 4, share, width), bf16),
        ],
        0,
        2 * block,
        name="pack_volume",
    )(volume.reshape(share, height, width))
    v_got = over_chan(v_out)
    own_sib, own_pair = to_sib(v_own), to_pair(v_own, True)
    u_own, *u_out = call(
        functools.partial(pack_rest_body, nchan, rows),
        [u_shape] * nchan,
        [
            pltpu.VMEM((share * height, width), f32),
            pltpu.VMEM((height + 2, share, width), bf16),
        ],
        0,
        3 * block,
        name="pack_rest",
    )(upstream.reshape(share, height, width), slabs, bias.reshape(1, share))
    v_got, own_pair = lax.optimization_barrier((v_got, own_pair))
    mine = [v_own] + v_got
    sib = [own_sib] + [to_sib(x) for x in v_got]
    pair = [own_pair] + [to_pair(x, True) for x in v_got]
    u_got = over_chan(u_out)
    w_backward = call(
        functools.partial(backward_filters_body, nchan, rows),
        shape(3 * full, 640),
        [pltpu.VMEM((nchan, 15, share, 128), bf16), pltpu.VMEM((640, 256), f32)],
        0,
        1 << 20,
        name="filters",
    )(u_own, *u_got)
    planes = pltpu.VMEM((rows + 4, 3, nchan, share, 128), bf16)
    cells = rows * width
    a_shape = shape(rows, share, 128)
    step = 4 if rows % 4 == 0 else 1
    h_shape = (nchan, 3 * share // 2, 640)
    *act, delta, kept, sent = call(
        functools.partial(forward_body, nchan, rows, step),
        [a_shape] * nchan
        + [shape(rows + 2, full, 128), shape(*h_shape, dtype=f32), shape(*h_shape)],
        [
            planes,
            pltpu.VMEM((rows + 2, nchan, share, 128), bf16),
            pltpu.VMEM((rows, nchan, share, 128), bf16),
            pltpu.VMEM((3 * full, 640), f32),
            pltpu.VMEM((nchan, 15, share, 128), bf16),
            pltpu.VMEM((3 * full, 640), bf16),
        ],
        4 * 27 * full * full * cells,
        8 * block,
        2 * full * cells,
        name="forward",
    )(*mine, *sib, *pair, u_own, *u_got)
    d_sib, d_pair = to_sib(delta), to_pair(delta, False)
    kept = kept + to_sib(sent).astype(f32)
    sent = [kept[k].astype(bf16) for k in range(nchan)]

    def from_hop(blocks, hop):
        got = [
            lax.ppermute(
                blocks[k],
                ("space", "chan"),
                [
                    (i * nchan + c, (i ^ hop) * nchan + (c + k) % nchan)
                    for i in range(nspace)
                    for c in range(nchan)
                ],
            )
            for k in range(len(blocks))
            if hop or k
        ]
        got = got if hop else [blocks[0]] + got
        return kept_sum(got[0], got[1:])

    def from_hops(blocks, hops):
        reach = [0]
        for hop in hops:
            reach += [hop ^ other for other in reach]
        sums = [from_hop(blocks, hop) for hop in reach]
        while len(sums) > 1:
            sums = [a + b for a, b in zip(sums[0::2], sums[1::2])]
        return sums[0]

    near = 4 if nspace > 4 else 2
    total = from_hops(sent, (near,))

    def unpack(blocks, name):
        out = call(
            functools.partial(unpack_body, nchan, rows, height),
            shape(share, height, width),
            [
                pltpu.VMEM((share, height, width), bf16),
                pltpu.VMEM((height * (share + 8), 128), f32),
                pltpu.SemaphoreType.DMA((4,)),
            ],
            0,
            2 * block,
            name=name,
            out_specs=pl.BlockSpec(memory_space=pl.ANY),
        )(*blocks)
        return out.reshape(share, 1, height, width)

    activated = unpack([act[0]] + over_chan(act[1:]), "unpack_activated")
    ig = call(
        functools.partial(backward_body, nchan, rows),
        [a_shape] * nchan,
        [pltpu.VMEM((rows, nchan, share, 128), bf16)],
        2 * 27 * full * full * cells,
        6 * block,
        name="backward",
    )(delta, d_sib, d_pair, w_backward)
    ig_got = over_chan(ig[1:])
    hops = [1 << n for n in range(1, nspace.bit_length() - 1) if 1 << n != near]
    for hop in hops[1:] + hops[:1]:
        total = from_hops([total.astype(bf16)], (hop,))
    summed = to_sib(total)

    input_grad = unpack([ig[0]] + ig_got, "unpack_input_grad")
    w_grad, b_grad = call(
        functools.partial(finish_body, share, factor),
        [shape(27, share, full, dtype=f32), shape(1, share, dtype=f32)],
        [pltpu.VMEM((3 * share, 640), f32)],
        0,
        1 << 20,
        name="finish",
    )(total, summed)
    w_grad = jnp.transpose(w_grad.reshape(3, 3, 3, share, full), (3, 4, 0, 1, 2))
    return activated, input_grad, w_grad, b_grad.reshape(share)


def solution(mesh):
    placed = (
        P("chan", "space", None, None),
        P("chan", None, None, None, None),
        P("chan"),
        P("chan", "space", None, None),
    )
    return jax.shard_map(
        shards,
        mesh=mesh,
        in_specs=placed,
        out_specs=(
            P("chan", "space", None, None),
            P("chan", "space", None, None),
            P("chan", None, None, None, None),
            P("chan"),
        ),
        check_vma=False,
    )
```

```python
import functools
import math

import jax
import jax.numpy as jnp
from jax import lax
from jax.experimental import pallas as pl
from jax.experimental.pallas import tpu as pltpu
from jax.sharding import PartitionSpec as P

leakage = 0.1
bf16 = jnp.bfloat16
f32 = jnp.float32
LIMIT = 48 * 1024 * 1024


def call(body, out_shape, scratch, flops, nbytes, trans=0, name=None, **specs):
    return pl.pallas_call(
        body,
        out_shape=out_shape,
        **specs,
        scratch_shapes=scratch,
        compiler_params=pltpu.CompilerParams(vmem_limit_bytes=LIMIT),
        cost_estimate=pl.CostEstimate(
            flops=flops, bytes_accessed=nbytes, transcendentals=trans
        ),
        name=name,
    )


def shape(*dims, dtype=bf16):
    return jax.ShapeDtypeStruct(dims, dtype)


def tap(a, b, c):
    return (a * 3 + b) * 3 + c


def rows_first(src, flat, dst, rim):
    share, height, _ = src.shape
    zero = jnp.zeros((rim, share, 128), bf16)
    pitch = height + 8
    for ch in range(share):
        flat[ch * pitch : ch * pitch + height] = src[ch].astype(f32)
    dst[0:rim] = zero
    dst[height + rim : height + 2 * rim] = zero
    for h in range(height):
        dst[h + rim] = flat[pl.ds(h, share, stride=pitch)].astype(bf16)


def pack_volume_body(nchan, rows, *refs):
    vol = refs[0]
    outs = refs[1 : 1 + nchan]
    flat, vt = refs[1 + nchan :]
    part = lax.axis_index("chan")
    rows_first(vol, flat, vt, 2)
    for k in range(nchan):
        outs[k][...] = vt[pl.ds(lax.rem(part + k, nchan) * rows, rows + 4)]


def core():
    return lax.rem(lax.axis_index("space"), 2)


def pack_rest_body(nchan, rows, *refs):
    up, w, bias = refs[:3]
    outs = refs[3 : 3 + nchan]
    flat, ut = refs[3 + nchan :]
    share = up.shape[0]
    part = lax.axis_index("chan")
    rows_first(up, flat, ut, 1)
    lane = lax.broadcasted_iota(jnp.int32, (share, 64), 1)
    row = lax.broadcasted_iota(jnp.int32, (share, share), 0)
    col = lax.broadcasted_iota(jnp.int32, (share, share), 1)
    b = jnp.sum(jnp.where(row == col, bias[...], 0.0), axis=1, keepdims=True)
    b0 = b.astype(bf16).astype(f32)
    b1 = (b - b0).astype(bf16).astype(f32)
    b2 = b - b0 - b1
    pieces = jnp.where(
        lane == 0, b0, jnp.where(lane == 1, b1, jnp.where(lane == 2, b2, 0.0))
    )
    none = jnp.zeros((share, 64), f32)
    for c in range(3):
        for j in range(5):
            halves = []
            for t in (2 * j, 2 * j + 1):
                if t < 9:
                    halves.append(w[tap(t % 3, t // 3, c)].astype(f32))
                else:
                    halves.append(pieces if c == 1 else none)
            value = jnp.concatenate(halves, axis=1).astype(bf16)
            for k in range(nchan):
                outs[k][rows + 2 + c * 5 + j] = value
    for k in range(nchan):
        outs[k][0 : rows + 2] = ut[pl.ds(lax.rem(part + k, nchan) * rows, rows + 2)]


def gather_filters(nchan, rows, wall, blocks):
    part = lax.axis_index("chan")
    for k in range(nchan):
        wall[lax.rem(part + nchan - k, nchan)] = blocks[k][rows + 2 :]


def backward_filters_body(nchan, rows, *refs):
    blocks = refs[:nchan]
    backward, wall, turned = refs[nchan:]
    full = nchan * blocks[0].shape[1]
    gather_filters(nchan, rows, wall, blocks)
    turned[...] = jnp.zeros_like(turned)
    for a in range(3):
        plane = 0 if a == 1 else 2 - core() if a == 0 else 1 + core()
        for b in range(3):
            at = pl.ds(pl.multiple_of((plane * 3 + b) * 64, 64), 64)
            t = (2 - b) * 3 + (2 - a)
            for c in range(3):
                block = wall[:, (2 - c) * 5 + t // 2].reshape(full, 128).astype(f32)
                half = block[:, (t % 2) * 64 : (t % 2) * 64 + 64]
                turned[at, c * 64 : (c + 1) * 64] = half

    @pl.when(outermost())
    def _():
        turned[6 * 64 : 9 * 64] = jnp.zeros((3 * 64, 256), f32)

    backward[...] = turned[...].T[: 3 * 64].astype(bf16)


def outermost():
    at = lax.axis_index("space")
    return (at == 0) | (at == lax.axis_size("space") - 1)


def gather_planes(nchan, planes, own, mine, sib, pair):
    part = lax.axis_index("chan")
    even = lax.rem(lax.axis_index("space"), 2) == 0
    at_sib = jnp.where(even, 2, 0)
    at_pair = jnp.where(even, 0, 2)
    for place, blocks in ((1, own), (at_sib, sib), (at_pair, pair)):
        for k in range(nchan):
            planes[:, place, lax.rem(part + nchan - k, nchan)] = blocks[k][...]

    @pl.when(outermost())
    def _():
        planes[:, at_pair] = jnp.zeros(planes[:, at_pair].shape, bf16)


def ones_rows(width):
    row = lax.broadcasted_iota(jnp.int32, (64, width), 0)
    return jnp.where(row < 3, 1.0, 0.0).astype(bf16)


def taps_of(planes, r, extra):
    block = planes[r : r + 3].reshape(-1, 128)
    return jnp.concatenate([block, extra], axis=0)


def shift_sum(y, full):
    lane = lax.broadcasted_iota(jnp.int32, (full, 128), 1)
    left = jnp.where(lane == 0, 0.0, pltpu.roll(y[:full], 1, 1))
    right = jnp.where(lane == 127, 0.0, pltpu.roll(y[2 * full :], 127, 1))
    return y[full : 2 * full] + left + right


def forward_body(nchan, rows, step, *refs):
    own, sib, pair = refs[:nchan], refs[nchan : 2 * nchan], refs[2 * nchan : 3 * nchan]
    ups = refs[3 * nchan : 4 * nchan]
    outs = refs[4 * nchan : 5 * nchan]
    delta, kept, sent, planes, upstream, activated, acc, wall, filters = refs[5 * nchan :]
    part = lax.axis_index("chan")
    share = own[0].shape[1]
    full = nchan * share
    gather_planes(nchan, planes, own, None, sib, pair)
    for k in range(nchan):
        upstream[:, lax.rem(part + nchan - k, nchan)] = ups[k][0 : rows + 2]
    gather_filters(nchan, rows, wall, ups)
    for c in range(3):
        for j in range(5):
            block = wall[:, c * 5 + j].reshape(full, 128)
            filters[c * full : (c + 1) * full, j * 128 : (j + 1) * 128] = block
    extra = ones_rows(128)
    w = filters[...]
    for g in range((rows + 2) // 2):
        rhs = jnp.concatenate(
            [taps_of(planes, 2 * g, extra), taps_of(planes, 2 * g + 1, extra)], axis=1
        )
        y = jnp.dot(w, rhs, preferred_element_type=f32)
        for n in range(2):
            r = 2 * g + n
            v = shift_sum(y[:, n * 128 : (n + 1) * 128], full)
            e = jnp.exp(-jnp.abs(v))
            inv = 1.0 / (1.0 + e)
            sig = jnp.where(v >= 0, 1.0, e) * inv
            u = upstream[r].reshape(full, 128).astype(f32)
            delta[r] = (u * (leakage + (1.0 - leakage) * sig)).astype(bf16)
            if 1 <= r <= rows:
                soft = jnp.maximum(v, 0.0) + jnp.log(1.0 + e)
                act = (leakage * v + (1.0 - leakage) * soft).astype(bf16)
                activated[r - 1] = act.reshape(nchan, share, 128)
    for k in range(nchan):
        outs[k][...] = activated[:, lax.rem(part + k, nchan)]
    lane = lax.broadcasted_iota(jnp.int32, (full, 128), 1)
    total = None
    for g in range(rows // step):
        lhs, rhs = [], []
        for r in range(g * step + 1, (g + 1) * step + 1):
            d = delta[r].astype(f32)
            before = jnp.where(lane == 127, 0.0, pltpu.roll(d, 127, 1))
            after = jnp.where(lane == 0, 0.0, pltpu.roll(d, 1, 1))
            lhs.append(
                jnp.concatenate([before.astype(bf16), delta[r], after.astype(bf16)], axis=0)
            )
            rhs.append(taps_of(planes, r, extra))
        term = lax.dot_general(
            jnp.concatenate(lhs, axis=1),
            jnp.concatenate(rhs, axis=1),
            (((1,), (1,)), ((), ())),
            preferred_element_type=f32,
        )
        total = term if total is None else total + term
    for c in range(3):
        for q in range(nchan):
            at = (q * 3 + c) * share
            acc[at : at + share] = total[c * full + q * share : c * full + (q + 1) * share]
    half = 3 * share // 2
    for k in range(nchan):
        at = lax.rem(part + k, nchan) * 3 * share
        kept[k] = acc[pl.ds(pl.multiple_of(at + core() * half, 8), half)]
        sent[k] = acc[pl.ds(pl.multiple_of(at + (1 - core()) * half, 8), half)].astype(bf16)


def backward_body(nchan, rows, *refs):
    sources, filters = refs[:3], refs[3]
    outs = refs[4 : 4 + nchan]
    result = refs[4 + nchan]
    part = lax.axis_index("chan")
    share = outs[0].shape[1]
    full = nchan * share
    extra = jnp.zeros((64, 128), bf16)

    def taps(r):
        blocks = [source[r : r + 3].reshape(-1, 128) for source in sources]
        return jnp.concatenate(blocks + [extra], axis=0)

    w = filters[...]
    for g in range(rows // 2):
        rhs = jnp.concatenate(
            [taps(2 * g), taps(2 * g + 1)], axis=1
        )
        y = jnp.dot(w, rhs, preferred_element_type=f32)
        for n in range(2):
            v = shift_sum(y[:, n * 128 : (n + 1) * 128], full)
            result[2 * g + n] = v.astype(bf16).reshape(nchan, share, 128)
    for k in range(nchan):
        outs[k][...] = result[:, lax.rem(part + k, nchan)]


def unpack_body(nchan, rows, height, *refs):
    blocks = refs[:nchan]
    out, staged, flat, sems = refs[nchan:]
    share = out.shape[0]
    part = lax.axis_index("chan")
    pitch = share + 8
    for k in range(nchan):
        q = lax.rem(part + nchan - k, nchan)
        for row in range(rows):
            at = pl.multiple_of(q * (rows * pitch) + row * pitch, 8)
            flat[pl.ds(at, share)] = blocks[k][row].astype(f32)
    copies = []
    for n in range(4):
        group = pl.ds(n * (share // 4), share // 4)
        for ch in range(n * (share // 4), (n + 1) * (share // 4)):
            staged[ch] = flat[pl.ds(ch, height, stride=pitch)].astype(bf16)
        copies.append(pltpu.make_async_copy(staged.at[group], out.at[group], sems.at[n]))
        copies[-1].start()
    for copy in copies:
        copy.wait()


def finish_body(share, factor, mine, other, out, bias, both):
    half = 3 * share // 2
    both[pl.ds(pl.multiple_of(core() * half, 8), half)] = mine[...]
    both[pl.ds(pl.multiple_of((1 - core()) * half, 8), half)] = other[...]
    total = both[...] * factor
    for a in range(3):
        for b in range(3):
            for c in range(3):
                t = b * 3 + a
                out[tap(a, b, c)] = total[c * share : (c + 1) * share, t * 64 : t * 64 + 64]
    col = total[share : 2 * share, 576:577]
    eye = lax.broadcasted_iota(jnp.int32, (share, share), 0) == lax.broadcasted_iota(
        jnp.int32, (share, share), 1
    )
    bias[...] = jnp.sum(jnp.where(eye, col, 0.0), axis=0, keepdims=True)


def kept_sum(first, others):
    total = first.astype(f32)
    for term in others:
        total = total + term.astype(f32)
    return total


def shards(volume, weight, bias, upstream):
    nchan, nspace = lax.axis_size("chan"), lax.axis_size("space")
    share, depth, height, width = volume.shape
    assert depth == 1 and width == 128 and height % nchan == 0
    full = nchan * share
    rows = height // nchan
    factor = 1.0 / math.sqrt(nspace * depth * height * width)
    sib_perm = [(i, i ^ 1) for i in range(nspace)]
    pairs = [(i, i + 1) for i in range(1, nspace - 1, 2)]
    pairs += [(j, i) for i, j in pairs]
    pair_perm = [(i * nchan + c, j * nchan + c) for i, j in pairs for c in range(nchan)]
    ends = (0, nspace - 1)
    turn_perm = [
        (i * nchan + c, i * nchan + (c + 1) % nchan) for i in ends for c in range(nchan)
    ]
    wrap_perm = [
        (i * nchan + c, (nspace - 1 - i) * nchan + c) for i in ends for c in range(nchan)
    ]

    def over_chan(blocks):
        got = []
        for k in range(1, nchan):
            perm = [(i, (i + k) % nchan) for i in range(nchan)]
            got.append(lax.ppermute(blocks[k - 1], "chan", perm))
        return got

    def to_sib(x):
        return lax.ppermute(x, "space", sib_perm)

    def to_pair(x, wrap):
        perm = pair_perm + (wrap_perm if wrap else turn_perm)
        return lax.ppermute(x, ("space", "chan"), perm)

    slabs = jnp.transpose(weight, (2, 3, 4, 0, 1)).reshape(27, share, full)
    block = share * height * width * 2
    v_shape = shape(rows + 4, share, 128)
    u_shape = shape(rows + 17, share, 128)
    v_own, *v_out = call(
        functools.partial(pack_volume_body, nchan, rows),
        [v_shape] * nchan,
        [
            pltpu.VMEM((share * (height + 8), width), f32),
            pltpu.VMEM((height + 4, share, width), bf16),
        ],
        0,
        2 * block,
        name="pack_volume",
    )(volume.reshape(share, height, width))
    v_got = over_chan(v_out)
    own_sib, own_pair = to_sib(v_own), to_pair(v_own, True)
    u_own, *u_out = call(
        functools.partial(pack_rest_body, nchan, rows),
        [u_shape] * nchan,
        [
            pltpu.VMEM((share * (height + 8), width), f32),
            pltpu.VMEM((height + 2, share, width), bf16),
        ],
        0,
        3 * block,
        name="pack_rest",
    )(upstream.reshape(share, height, width), slabs, bias.reshape(1, share))
    v_got, own_pair = lax.optimization_barrier((v_got, own_pair))
    mine = [v_own] + v_got
    sib = [own_sib] + [to_sib(x) for x in v_got]
    pair = [own_pair] + [to_pair(x, True) for x in v_got]
    u_got = over_chan(u_out)
    w_backward = call(
        functools.partial(backward_filters_body, nchan, rows),
        shape(3 * full, 640),
        [pltpu.VMEM((nchan, 15, share, 128), bf16), pltpu.VMEM((640, 256), f32)],
        0,
        1 << 20,
        name="filters",
    )(u_own, *u_got)
    planes = pltpu.VMEM((rows + 4, 3, nchan, share, 128), bf16)
    cells = rows * width
    a_shape = shape(rows, share, 128)
    step = 4 if rows % 4 == 0 else 1
    h_shape = (nchan, 3 * share // 2, 640)
    *act, delta, kept, sent = call(
        functools.partial(forward_body, nchan, rows, step),
        [a_shape] * nchan
        + [shape(rows + 2, full, 128), shape(*h_shape, dtype=f32), shape(*h_shape)],
        [
            planes,
            pltpu.VMEM((rows + 2, nchan, share, 128), bf16),
            pltpu.VMEM((rows, nchan, share, 128), bf16),
            pltpu.VMEM((3 * full, 640), f32),
            pltpu.VMEM((nchan, 15, share, 128), bf16),
            pltpu.VMEM((3 * full, 640), bf16),
        ],
        4 * 27 * full * full * cells,
        8 * block,
        2 * full * cells,
        name="forward",
    )(*mine, *sib, *pair, u_own, *u_got)
    d_sib, d_pair = to_sib(delta), to_pair(delta, False)
    kept = kept + to_sib(sent).astype(f32)
    sent = [kept[k].astype(bf16) for k in range(nchan)]

    def from_hop(blocks, hop):
        got = [
            lax.ppermute(
                blocks[k],
                ("space", "chan"),
                [
                    (i * nchan + c, (i ^ hop) * nchan + (c + k) % nchan)
                    for i in range(nspace)
                    for c in range(nchan)
                ],
            )
            for k in range(len(blocks))
            if hop or k
        ]
        got = got if hop else [blocks[0]] + got
        return kept_sum(got[0], got[1:])

    def from_hops(blocks, hops):
        reach = [0]
        for hop in hops:
            reach += [hop ^ other for other in reach]
        sums = [from_hop(blocks, hop) for hop in reach]
        while len(sums) > 1:
            sums = [a + b for a, b in zip(sums[0::2], sums[1::2])]
        return sums[0]

    near = 4 if nspace > 4 else 2
    total = from_hops(sent, (near,))

    def unpack(blocks, name):
        out = call(
            functools.partial(unpack_body, nchan, rows, height),
            shape(share, height, width),
            [
                pltpu.VMEM((share, height, width), bf16),
                pltpu.VMEM((height * (share + 8), 128), f32),
                pltpu.SemaphoreType.DMA((4,)),
            ],
            0,
            2 * block,
            name=name,
            out_specs=pl.BlockSpec(memory_space=pl.ANY),
        )(*blocks)
        return out.reshape(share, 1, height, width)

    activated = unpack([act[0]] + over_chan(act[1:]), "unpack_activated")
    ig = call(
        functools.partial(backward_body, nchan, rows),
        [a_shape] * nchan,
        [pltpu.VMEM((rows, nchan, share, 128), bf16)],
        2 * 27 * full * full * cells,
        6 * block,
        name="backward",
    )(delta, d_sib, d_pair, w_backward)
    ig_got = over_chan(ig[1:])
    hops = [1 << n for n in range(1, nspace.bit_length() - 1) if 1 << n != near]
    for hop in hops[1:] + hops[:1]:
        total = from_hops([total.astype(bf16)], (hop,))
    summed = to_sib(total)

    input_grad = unpack([ig[0]] + ig_got, "unpack_input_grad")
    w_grad, b_grad = call(
        functools.partial(finish_body, share, factor),
        [shape(27, share, full, dtype=f32), shape(1, share, dtype=f32)],
        [pltpu.VMEM((3 * share, 640), f32)],
        0,
        1 << 20,
        name="finish",
    )(total, summed)
    w_grad = jnp.transpose(w_grad.reshape(3, 3, 3, share, full), (3, 4, 0, 1, 2))
    return activated, input_grad, w_grad, b_grad.reshape(share)


def solution(mesh):
    placed = (
        P("chan", "space", None, None),
        P("chan", None, None, None, None),
        P("chan"),
        P("chan", "space", None, None),
    )
    return jax.shard_map(
        shards,
        mesh=mesh,
        in_specs=placed,
        out_specs=(
            P("chan", "space", None, None),
            P("chan", "space", None, None),
            P("chan", None, None, None, None),
            P("chan"),
        ),
        check_vma=False,
    )
```

```python
import functools
import math

import jax
import jax.numpy as jnp
from jax import lax
from jax.experimental import pallas as pl
from jax.experimental.pallas import tpu as pltpu
from jax.sharding import PartitionSpec as P

leakage = 0.1
bf16 = jnp.bfloat16
f32 = jnp.float32
LIMIT = 48 * 1024 * 1024


def call(body, out_shape, scratch, flops, nbytes, trans=0, name=None, **specs):
    return pl.pallas_call(
        body,
        out_shape=out_shape,
        **specs,
        scratch_shapes=scratch,
        compiler_params=pltpu.CompilerParams(vmem_limit_bytes=LIMIT),
        cost_estimate=pl.CostEstimate(
            flops=flops, bytes_accessed=nbytes, transcendentals=trans
        ),
        name=name,
    )


def shape(*dims, dtype=bf16):
    return jax.ShapeDtypeStruct(dims, dtype)


def tap(a, b, c):
    return (a * 3 + b) * 3 + c


def rows_first(src, flat, dst, rim):
    share, height, _ = src.shape
    zero = jnp.zeros((rim, share, 128), bf16)
    pitch = height + 8
    for ch in range(share):
        flat[ch * pitch : ch * pitch + height] = src[ch].astype(f32)
    dst[0:rim] = zero
    dst[height + rim : height + 2 * rim] = zero
    for h in range(height):
        dst[h + rim] = flat[pl.ds(h, share, stride=pitch)].astype(bf16)


def pack_volume_body(nchan, rows, *refs):
    vol = refs[0]
    outs = refs[1 : 1 + nchan]
    flat, vt = refs[1 + nchan :]
    part = lax.axis_index("chan")
    rows_first(vol, flat, vt, 2)
    for k in range(nchan):
        outs[k][...] = vt[pl.ds(lax.rem(part + k, nchan) * rows, rows + 4)]


def core():
    return lax.rem(lax.axis_index("space"), 2)


def pack_rest_body(nchan, rows, *refs):
    up, w, bias = refs[:3]
    outs = refs[3 : 3 + nchan]
    flat, ut = refs[3 + nchan :]
    share = up.shape[0]
    part = lax.axis_index("chan")
    rows_first(up, flat, ut, 1)
    lane = lax.broadcasted_iota(jnp.int32, (share, 64), 1)
    row = lax.broadcasted_iota(jnp.int32, (share, share), 0)
    col = lax.broadcasted_iota(jnp.int32, (share, share), 1)
    b = jnp.sum(jnp.where(row == col, bias[...], 0.0), axis=1, keepdims=True)
    b0 = b.astype(bf16).astype(f32)
    b1 = (b - b0).astype(bf16).astype(f32)
    b2 = b - b0 - b1
    pieces = jnp.where(
        lane == 0, b0, jnp.where(lane == 1, b1, jnp.where(lane == 2, b2, 0.0))
    )
    none = jnp.zeros((share, 64), f32)
    for c in range(3):
        for j in range(5):
            halves = []
            for t in (2 * j, 2 * j + 1):
                if t < 9:
                    halves.append(w[tap(t % 3, t // 3, c)].astype(f32))
                else:
                    halves.append(pieces if c == 1 else none)
            value = jnp.concatenate(halves, axis=1).astype(bf16)
            for k in range(nchan):
                outs[k][rows + 2 + c * 5 + j] = value
    for k in range(nchan):
        outs[k][0 : rows + 2] = ut[pl.ds(lax.rem(part + k, nchan) * rows, rows + 2)]


def gather_filters(nchan, rows, wall, blocks):
    part = lax.axis_index("chan")
    for k in range(nchan):
        wall[lax.rem(part + nchan - k, nchan)] = blocks[k][rows + 2 :]


def backward_filters_body(nchan, rows, *refs):
    blocks = refs[:nchan]
    backward, wall, turned = refs[nchan:]
    full = nchan * blocks[0].shape[1]
    gather_filters(nchan, rows, wall, blocks)
    turned[...] = jnp.zeros_like(turned)
    for a in range(3):
        plane = 0 if a == 1 else 2 - core() if a == 0 else 1 + core()
        for b in range(3):
            at = pl.ds(pl.multiple_of((plane * 3 + b) * 64, 64), 64)
            t = (2 - b) * 3 + (2 - a)
            for c in range(3):
                block = wall[:, (2 - c) * 5 + t // 2].reshape(full, 128).astype(f32)
                half = block[:, (t % 2) * 64 : (t % 2) * 64 + 64]
                turned[at, c * 64 : (c + 1) * 64] = half

    @pl.when(outermost())
    def _():
        turned[6 * 64 : 9 * 64] = jnp.zeros((3 * 64, 256), f32)

    backward[...] = turned[...].T[: 3 * 64].astype(bf16)


def outermost():
    at = lax.axis_index("space")
    return (at == 0) | (at == lax.axis_size("space") - 1)


def gather_planes(nchan, planes, own, mine, sib, pair):
    part = lax.axis_index("chan")
    even = lax.rem(lax.axis_index("space"), 2) == 0
    at_sib = jnp.where(even, 2, 0)
    at_pair = jnp.where(even, 0, 2)
    for place, blocks in ((1, own), (at_sib, sib), (at_pair, pair)):
        for k in range(nchan):
            planes[:, place, lax.rem(part + nchan - k, nchan)] = blocks[k][...]

    @pl.when(outermost())
    def _():
        planes[:, at_pair] = jnp.zeros(planes[:, at_pair].shape, bf16)


def ones_rows(width):
    row = lax.broadcasted_iota(jnp.int32, (64, width), 0)
    return jnp.where(row < 3, 1.0, 0.0).astype(bf16)


def taps_of(planes, r, extra):
    block = planes[r : r + 3].reshape(-1, 128)
    return jnp.concatenate([block, extra], axis=0)


def shift_sum(y, full):
    lane = lax.broadcasted_iota(jnp.int32, (full, 128), 1)
    left = jnp.where(lane == 0, 0.0, pltpu.roll(y[:full], 1, 1))
    right = jnp.where(lane == 127, 0.0, pltpu.roll(y[2 * full :], 127, 1))
    return y[full : 2 * full] + left + right


def forward_body(nchan, rows, step, *refs):
    own, sib, pair = refs[:nchan], refs[nchan : 2 * nchan], refs[2 * nchan : 3 * nchan]
    ups = refs[3 * nchan : 4 * nchan]
    outs = refs[4 * nchan : 5 * nchan]
    delta, kept, sent, planes, upstream, activated, acc, wall, filters = refs[5 * nchan :]
    part = lax.axis_index("chan")
    share = own[0].shape[1]
    full = nchan * share
    gather_planes(nchan, planes, own, None, sib, pair)
    for k in range(nchan):
        upstream[:, lax.rem(part + nchan - k, nchan)] = ups[k][0 : rows + 2]
    gather_filters(nchan, rows, wall, ups)
    for c in range(3):
        for j in range(5):
            block = wall[:, c * 5 + j].reshape(full, 128)
            filters[c * full : (c + 1) * full, j * 128 : (j + 1) * 128] = block
    extra = ones_rows(128)
    w = filters[...]
    for g in range((rows + 2) // 2):
        rhs = jnp.concatenate(
            [taps_of(planes, 2 * g, extra), taps_of(planes, 2 * g + 1, extra)], axis=1
        )
        y = jnp.dot(w, rhs, preferred_element_type=f32)
        for n in range(2):
            r = 2 * g + n
            v = shift_sum(y[:, n * 128 : (n + 1) * 128], full)
            e = jnp.exp(-jnp.abs(v))
            inv = 1.0 / (1.0 + e)
            sig = jnp.where(v >= 0, 1.0, e) * inv
            u = upstream[r].reshape(full, 128).astype(f32)
            delta[r] = (u * (leakage + (1.0 - leakage) * sig)).astype(bf16)
            if 1 <= r <= rows:
                soft = jnp.maximum(v, 0.0) + jnp.log(1.0 + e)
                act = (leakage * v + (1.0 - leakage) * soft).astype(bf16)
                activated[r - 1] = act.reshape(nchan, share, 128)
    for k in range(nchan):
        outs[k][...] = activated[:, lax.rem(part + k, nchan)]
    lane = lax.broadcasted_iota(jnp.int32, (full, 128), 1)
    total = None
    for g in range(rows // step):
        lhs, rhs = [], []
        for r in range(g * step + 1, (g + 1) * step + 1):
            d = delta[r].astype(f32)
            before = jnp.where(lane == 127, 0.0, pltpu.roll(d, 127, 1))
            after = jnp.where(lane == 0, 0.0, pltpu.roll(d, 1, 1))
            lhs.append(
                jnp.concatenate([before.astype(bf16), delta[r], after.astype(bf16)], axis=0)
            )
            rhs.append(taps_of(planes, r, extra))
        term = lax.dot_general(
            jnp.concatenate(lhs, axis=1),
            jnp.concatenate(rhs, axis=1),
            (((1,), (1,)), ((), ())),
            preferred_element_type=f32,
        )
        total = term if total is None else total + term
    for c in range(3):
        for q in range(nchan):
            at = (q * 3 + c) * share
            acc[at : at + share] = total[c * full + q * share : c * full + (q + 1) * share]
    half = 3 * share // 2
    for k in range(nchan):
        at = lax.rem(part + k, nchan) * 3 * share
        kept[k] = acc[pl.ds(pl.multiple_of(at + core() * half, 8), half)]
        sent[k] = acc[pl.ds(pl.multiple_of(at + (1 - core()) * half, 8), half)].astype(bf16)


def backward_body(nchan, rows, *refs):
    sources, filters = refs[:3], refs[3]
    outs = refs[4 : 4 + nchan]
    result = refs[4 + nchan]
    part = lax.axis_index("chan")
    share = outs[0].shape[1]
    full = nchan * share
    extra = jnp.zeros((64, 128), bf16)

    def taps(r):
        blocks = [source[r : r + 3].reshape(-1, 128) for source in sources]
        return jnp.concatenate(blocks + [extra], axis=0)

    w = filters[...]
    for g in range(rows // 2):
        rhs = jnp.concatenate(
            [taps(2 * g), taps(2 * g + 1)], axis=1
        )
        y = jnp.dot(w, rhs, preferred_element_type=f32)
        for n in range(2):
            v = shift_sum(y[:, n * 128 : (n + 1) * 128], full)
            result[2 * g + n] = v.astype(bf16).reshape(nchan, share, 128)
    for k in range(nchan):
        outs[k][...] = result[:, lax.rem(part + k, nchan)]


def unpack_body(nchan, rows, height, *refs):
    blocks = refs[:nchan]
    out, staged, flat, sems = refs[nchan:]
    share = out.shape[0]
    part = lax.axis_index("chan")
    pitch = share + 8
    for k in range(nchan):
        q = lax.rem(part + nchan - k, nchan)
        for row in range(rows):
            at = pl.multiple_of(q * (rows * pitch) + row * pitch, 8)
            flat[pl.ds(at, share)] = blocks[k][row].astype(f32)
    copies = []
    for n in range(4):
        group = pl.ds(n * (share // 4), share // 4)
        for ch in range(n * (share // 4), (n + 1) * (share // 4)):
            staged[ch] = flat[pl.ds(ch, height, stride=pitch)].astype(bf16)
        copies.append(pltpu.make_async_copy(staged.at[group], out.at[group], sems.at[n]))
        copies[-1].start()
    for copy in copies:
        copy.wait()


def finish_body(share, factor, mine, other, out, bias, both):
    half = 3 * share // 2
    both[pl.ds(pl.multiple_of(core() * half, 8), half)] = mine[...]
    both[pl.ds(pl.multiple_of((1 - core()) * half, 8), half)] = other[...]
    total = both[...] * factor
    for a in range(3):
        for b in range(3):
            for c in range(3):
                t = b * 3 + a
                out[tap(a, b, c)] = total[c * share : (c + 1) * share, t * 64 : t * 64 + 64]
    col = total[share : 2 * share, 576:577]
    eye = lax.broadcasted_iota(jnp.int32, (share, share), 0) == lax.broadcasted_iota(
        jnp.int32, (share, share), 1
    )
    bias[...] = jnp.sum(jnp.where(eye, col, 0.0), axis=0, keepdims=True)


def kept_sum(first, others):
    total = first.astype(f32)
    for term in others:
        total = total + term.astype(f32)
    return total


def shards(volume, weight, bias, upstream):
    nchan, nspace = lax.axis_size("chan"), lax.axis_size("space")
    share, depth, height, width = volume.shape
    assert depth == 1 and width == 128 and height % nchan == 0
    full = nchan * share
    rows = height // nchan
    factor = 1.0 / math.sqrt(nspace * depth * height * width)
    sib_perm = [(i, i ^ 1) for i in range(nspace)]
    pairs = [(i, i + 1) for i in range(1, nspace - 1, 2)]
    pairs += [(j, i) for i, j in pairs]
    pair_perm = [(i * nchan + c, j * nchan + c) for i, j in pairs for c in range(nchan)]
    ends = (0, nspace - 1)
    turn_perm = [
        (i * nchan + c, i * nchan + (c + 1) % nchan) for i in ends for c in range(nchan)
    ]
    wrap_perm = [
        (i * nchan + c, (nspace - 1 - i) * nchan + c) for i in ends for c in range(nchan)
    ]

    def over_chan(blocks):
        got = []
        for k in range(1, nchan):
            perm = [(i, (i + k) % nchan) for i in range(nchan)]
            got.append(lax.ppermute(blocks[k - 1], "chan", perm))
        return got

    def to_sib(x):
        return lax.ppermute(x, "space", sib_perm)

    def to_pair(x, wrap):
        perm = pair_perm + (wrap_perm if wrap else turn_perm)
        return lax.ppermute(x, ("space", "chan"), perm)

    slabs = jnp.transpose(weight, (2, 3, 4, 0, 1)).reshape(27, share, full)
    block = share * height * width * 2
    v_shape = shape(rows + 4, share, 128)
    u_shape = shape(rows + 17, share, 128)
    v_own, *v_out = call(
        functools.partial(pack_volume_body, nchan, rows),
        [v_shape] * nchan,
        [
            pltpu.VMEM((share * (height + 8), width), f32),
            pltpu.VMEM((height + 4, share, width), bf16),
        ],
        0,
        2 * block,
        name="pack_volume",
    )(volume.reshape(share, height, width))
    v_got = over_chan(v_out)
    own_sib, own_pair = to_sib(v_own), to_pair(v_own, True)
    u_own, *u_out = call(
        functools.partial(pack_rest_body, nchan, rows),
        [u_shape] * nchan,
        [
            pltpu.VMEM((share * (height + 8), width), f32),
            pltpu.VMEM((height + 2, share, width), bf16),
        ],
        0,
        3 * block,
        name="pack_rest",
    )(upstream.reshape(share, height, width), slabs, bias.reshape(1, share))
    v_got, own_pair = lax.optimization_barrier((v_got, own_pair))
    mine = [v_own] + v_got
    sib = [own_sib] + [to_sib(x) for x in v_got]
    pair = [own_pair] + [to_pair(x, True) for x in v_got]
    u_got = over_chan(u_out)
    w_backward = call(
        functools.partial(backward_filters_body, nchan, rows),
        shape(3 * full, 640),
        [pltpu.VMEM((nchan, 15, share, 128), bf16), pltpu.VMEM((640, 256), f32)],
        0,
        1 << 20,
        name="filters",
    )(u_own, *u_got)
    planes = pltpu.VMEM((rows + 4, 3, nchan, share, 128), bf16)
    cells = rows * width
    a_shape = shape(rows, share, 128)
    step = 4 if rows % 4 == 0 else 1
    h_shape = (nchan, 3 * share // 2, 640)
    *act, delta, kept, sent = call(
        functools.partial(forward_body, nchan, rows, step),
        [a_shape] * nchan
        + [shape(rows + 2, full, 128), shape(*h_shape, dtype=f32), shape(*h_shape)],
        [
            planes,
            pltpu.VMEM((rows + 2, nchan, share, 128), bf16),
            pltpu.VMEM((rows, nchan, share, 128), bf16),
            pltpu.VMEM((3 * full, 640), f32),
            pltpu.VMEM((nchan, 15, share, 128), bf16),
            pltpu.VMEM((3 * full, 640), bf16),
        ],
        4 * 27 * full * full * cells,
        8 * block,
        2 * full * cells,
        name="forward",
    )(*mine, *sib, *pair, u_own, *u_got)
    d_sib, d_pair = to_sib(delta), to_pair(delta, False)
    kept = kept + to_sib(sent).astype(f32)
    sent = [kept[k].astype(bf16) for k in range(nchan)]

    def from_hop(blocks, hop):
        got = [
            lax.ppermute(
                blocks[k],
                ("space", "chan"),
                [
                    (i * nchan + c, (i ^ hop) * nchan + (c + k) % nchan)
                    for i in range(nspace)
                    for c in range(nchan)
                ],
            )
            for k in range(len(blocks))
            if hop or k
        ]
        got = got if hop else [blocks[0]] + got
        return kept_sum(got[0], got[1:])

    def from_hops(blocks, hops):
        reach = [0]
        for hop in hops:
            reach += [hop ^ other for other in reach]
        sums = [from_hop(blocks, hop) for hop in reach]
        while len(sums) > 1:
            sums = [a + b for a, b in zip(sums[0::2], sums[1::2])]
        return sums[0]

    near = 2
    total = from_hops(sent, (near,))

    def unpack(blocks, name):
        out = call(
            functools.partial(unpack_body, nchan, rows, height),
            shape(share, height, width),
            [
                pltpu.VMEM((share, height, width), bf16),
                pltpu.VMEM((height * (share + 8), 128), f32),
                pltpu.SemaphoreType.DMA((4,)),
            ],
            0,
            2 * block,
            name=name,
            out_specs=pl.BlockSpec(memory_space=pl.ANY),
        )(*blocks)
        return out.reshape(share, 1, height, width)

    activated = unpack([act[0]] + over_chan(act[1:]), "unpack_activated")
    ig = call(
        functools.partial(backward_body, nchan, rows),
        [a_shape] * nchan,
        [pltpu.VMEM((rows, nchan, share, 128), bf16)],
        2 * 27 * full * full * cells,
        6 * block,
        name="backward",
    )(delta, d_sib, d_pair, w_backward)
    ig_got = over_chan(ig[1:])
    hops = [1 << n for n in range(1, nspace.bit_length() - 1) if 1 << n != near]
    for hop in hops:
        total = from_hops([total.astype(bf16)], (hop,))
    summed = to_sib(total)

    input_grad = unpack([ig[0]] + ig_got, "unpack_input_grad")
    w_grad, b_grad = call(
        functools.partial(finish_body, share, factor),
        [shape(27, share, full, dtype=f32), shape(1, share, dtype=f32)],
        [pltpu.VMEM((3 * share, 640), f32)],
        0,
        1 << 20,
        name="finish",
    )(total, summed)
    w_grad = jnp.transpose(w_grad.reshape(3, 3, 3, share, full), (3, 4, 0, 1, 2))
    return activated, input_grad, w_grad, b_grad.reshape(share)


def solution(mesh):
    placed = (
        P("chan", "space", None, None),
        P("chan", None, None, None, None),
        P("chan"),
        P("chan", "space", None, None),
    )
    return jax.shard_map(
        shards,
        mesh=mesh,
        in_specs=placed,
        out_specs=(
            P("chan", "space", None, None),
            P("chan", "space", None, None),
            P("chan", None, None, None, None),
            P("chan"),
        ),
        check_vma=False,
    )
```
